512 devices in a mesh: grp: 32 (over y, x, core), seq: 16 (over z).
Axes of the slice: x: 4, y: 4, z: 16, core: 2. Of those that a mesh axis runs over, the one named last changes fastest.
Arguments:
- q_space: bfloat16 [512, 256, 576], P(('grp', 'seq')), may hold values from -96 to 96
- k_space: bfloat16 [512, 256, 576], P(('grp', 'seq')), may hold values from -96 to 96
- v_space: bfloat16 [512, 256, 576], P(('grp', 'seq')), may hold values from -6 to 6
- cot_space: bfloat16 [512, 256, 576], P(('grp', 'seq')), may hold values from -6 to 6
- q_time: bfloat16 [512, 256, 576], P(('grp', 'seq')), may hold values from -96 to 96
- k_time: bfloat16 [512, 256, 576], P(('grp', 'seq')), may hold values from -96 to 96
- v_time: bfloat16 [512, 256, 576], P(('grp', 'seq')), may hold values from -6 to 6
- cot_time: bfloat16 [512, 256, 576], P(('grp', 'seq')), may hold values from -6 to 6
- clip_len: int32 [64], replicated, may hold values from 1 to 16, 512 in all
Outputs:
- grad_q_space: bfloat16 [512, 256, 576], P(('grp', 'seq'))
- grad_k_space: bfloat16 [512, 256, 576], P(('grp', 'seq'))
- grad_v_space: bfloat16 [512, 256, 576], P(('grp', 'seq'))
- grad_q_time: bfloat16 [512, 256, 576], P(('grp', 'seq'))
- grad_k_time: bfloat16 [512, 256, 576], P(('grp', 'seq'))
- grad_v_time: bfloat16 [512, 256, 576], P(('grp', 'seq'))
The draws below stay inside these ranges and needn't reach their ends.
Inputs may be any that keep to these rules, and one draw needn't show every extreme that they name: `clip_len`: the 64 frame counts sum to 512; some clip has exactly 16 frames.
All inputs are finite; a program needn't handle non-finite values.
Results may differ from the reference program's by a relative error of at most 0.013.
Values may be sent and summed in bfloat16 or wider, within the bound.
A program may use at most 64 MiB of HBM per device.

```python
import math
import jax
import jax.numpy as jnp
import numpy as np
from jax import lax

HEADS = 8
HDIM = 72
S = 256
WIN = 16
FRAMES = 512
CLIPS = 64
N_GRP = 32


def paired(key, salt):
    key = jax.random.fold_in(key, salt)
    full_shape = (FRAMES, S, HEADS * HDIM)
    pieces = jax.random.split(key, 2)
    queries = jnp.clip(jax.random.normal(pieces[0], full_shape, jnp.float32), -6.0, 6.0)
    keys = jnp.clip(jax.random.normal(pieces[1], full_shape, jnp.float32), -6.0, 6.0)
    return (queries, keys)


def draw_q_space(key, part):
    queries, keys = paired(key, 11)
    return queries.astype(jnp.bfloat16)


def draw_k_space(key, part):
    queries, keys = paired(key, 11)
    return keys.astype(jnp.bfloat16)


def draw_q_time(key, part):
    queries, keys = paired(key, 12)
    return queries.astype(jnp.bfloat16)


def draw_k_time(key, part):
    queries, keys = paired(key, 12)
    return keys.astype(jnp.bfloat16)


def steps_of(stream_key, dims, cuts, low, largest):
    loudness = 1.0
    for dim, parts in cuts:
        steps = jax.random.uniform(jax.random.fold_in(jax.random.fold_in(stream_key, 6), dim), (parts,), jnp.float32, low / len(cuts), largest / len(cuts))
        loudness = loudness * jnp.repeat(jnp.exp(steps), dims[dim] // parts).reshape((-1,) + (1,) * (len(dims) - 1 - dim))
    return loudness


def profile(number_of, total, reach, slope):
    loads = [(1 << 20) // math.isqrt(standing ** slope) + 1 for standing in range(2, number_of + 1)]
    rest, given = total - reach - (number_of - 1), [1] * (number_of - 1)
    while rest > 0:
        candidates = [i for i in range(number_of - 1) if given[i] < reach]
        whole, remaining = sum([loads[i] for i in candidates]), rest
        for i in candidates:
            extra = min(reach - given[i], max(1, remaining * loads[i] // whole), rest)
            given[i] = given[i] + extra
            rest = rest - extra
    return np.array([reach] + given)


def ragged_sizes(own_key, amount, total, bound, lean):
    if amount == 2:
        one = jax.random.randint(own_key, (), max(1, total - bound), min(bound, total - 1) + 1)
        return jnp.stack([one, total - one])
    tallies = jnp.asarray(profile(amount, total, bound, lean), jnp.int32)
    pairs = (amount - 1) // 2
    giver, receiver = tallies[1:1 + 2 * pairs:2], tallies[2:2 + 2 * pairs:2]
    slack = jnp.minimum(giver - 1, bound - receiver)
    passed = jax.random.randint(jax.random.fold_in(own_key, 1), (pairs,), 0, 1 << 20) % (slack + 1)
    tallies = tallies.at[1:1 + 2 * pairs:2].set(giver - passed).at[2:2 + 2 * pairs:2].set(receiver + passed)
    return tallies[jax.random.permutation(jax.random.fold_in(own_key, 2), amount)]


def gaussian(own_key, shape, width, bound, cuts=(), kind=jnp.bfloat16):
    entries = jax.random.normal(own_key, shape, jnp.float32) * width
    if len(cuts) > 0:
        entries = steps_of(own_key, shape, cuts, -0.22, 0.18) * entries
    return jnp.clip(entries, min=-bound, max=bound).astype(kind)


def setup_inputs(seed: int = 0) -> dict:
    key_list = jax.random.split(jax.random.key(seed), 10)
    q_space = draw_q_space(jax.random.fold_in(key_list[9], 71), 0)
    k_space = draw_k_space(jax.random.fold_in(key_list[9], 71), 0)
    v_space = gaussian(key_list[2], (FRAMES, S, HEADS * HDIM), 1.0, 6.0, ((0, 512),))
    cot_space = gaussian(key_list[3], (FRAMES, S, HEADS * HDIM), 1.0, 6.0, ((0, 512),))
    q_time = draw_q_time(jax.random.fold_in(key_list[9], 71), 0)
    k_time = draw_k_time(jax.random.fold_in(key_list[9], 71), 0)
    v_time = gaussian(key_list[6], (FRAMES, S, HEADS * HDIM), 1.0, 6.0, ((0, 512),))
    cot_time = gaussian(key_list[7], (FRAMES, S, HEADS * HDIM), 1.0, 6.0, ((0, 512),))
    clip_len = ragged_sizes(key_list[8], CLIPS, FRAMES, WIN, 2).astype(jnp.int32)
    return {"q_space": q_space, "k_space": k_space, "v_space": v_space, "cot_space": cot_space, "q_time": q_time, "k_time": k_time, "v_time": v_time, "cot_time": cot_time, "clip_len": clip_len}


masked_score = -1e+30

def rounded(array):
    return lax.optimization_barrier(array.astype(jnp.bfloat16)).astype(jnp.float32)

def split_heads(array):
    return array.astype(jnp.float32).reshape(array.shape[0], array.shape[1], HEADS, HDIM)

def clip_labels(clip_len, first_frame, count, frame_total):
    frame_ids = first_frame + jnp.arange(count, dtype=jnp.int32)
    clip_ends = jnp.cumsum(clip_len).astype(jnp.int32)
    labels = lax.optimization_barrier(jnp.sum((clip_ends[None, :] <= frame_ids[:, None]).astype(jnp.int32), axis=1))
    inside = (frame_ids >= 0) & (frame_ids < frame_total)
    return (labels, inside)

def frame_grads(operands):
    queries, keys, values, cotangent = operands
    scaling = 1.0 / math.sqrt(HDIM)
    q_heads = queries.astype(jnp.float32).reshape(S, HEADS, HDIM)
    k_heads = keys.astype(jnp.float32).reshape(S, HEADS, HDIM)
    v_heads = values.astype(jnp.float32).reshape(S, HEADS, HDIM)
    g_heads = cotangent.astype(jnp.float32).reshape(S, HEADS, HDIM)
    scores = jnp.einsum('qhd,khd->hqk', q_heads, k_heads) * scaling
    row_max = lax.optimization_barrier(jnp.max(scores, axis=-1, keepdims=True))
    log_total = row_max + jnp.log(lax.optimization_barrier(jnp.sum(jnp.exp(scores - row_max), axis=-1, keepdims=True)))
    weights = jnp.exp(scores - log_total)
    weights_low = rounded(weights)
    attended = jnp.einsum('hqk,khd->qhd', weights_low, v_heads)
    row_dot = jnp.einsum('qhd,qhd->hq', g_heads, attended)
    weight_grad = jnp.einsum('qhd,khd->hqk', g_heads, v_heads)
    score_grad = rounded(weights * (weight_grad - row_dot[:, :, None]))
    grad_query = jnp.einsum('hqk,khd->qhd', score_grad, k_heads) * scaling
    grad_key = jnp.einsum('hqk,qhd->khd', score_grad, q_heads) * scaling
    grad_value = jnp.einsum('hqk,qhd->khd', weights_low, g_heads)
    flat_shape = (S, HEADS * HDIM)
    return (grad_query.reshape(flat_shape).astype(jnp.bfloat16), grad_key.reshape(flat_shape).astype(jnp.bfloat16), grad_value.reshape(flat_shape).astype(jnp.bfloat16))

def time_grads(q_time, k_time, v_time, cot_time, clip_len):
    scaling = 1.0 / math.sqrt(HDIM)
    margin = ((WIN, WIN), (0, 0), (0, 0))
    key_pad = jnp.pad(k_time, margin)
    value_pad = jnp.pad(v_time, margin)
    query_pad = jnp.pad(q_time, margin)
    cot_pad = jnp.pad(cot_time, margin)

    def query_side(group_id):
        first_frame = group_id * WIN
        q_own = split_heads(lax.dynamic_slice_in_dim(q_time, first_frame, WIN, 0))
        g_own = split_heads(lax.dynamic_slice_in_dim(cot_time, first_frame, WIN, 0))
        k_ext = split_heads(lax.dynamic_slice_in_dim(key_pad, first_frame, 3 * WIN, 0))
        v_ext = split_heads(lax.dynamic_slice_in_dim(value_pad, first_frame, 3 * WIN, 0))
        own_label, own_inside = clip_labels(clip_len, first_frame, WIN, FRAMES)
        ext_label, ext_inside = clip_labels(clip_len, first_frame - WIN, 3 * WIN, FRAMES)
        allowed = (own_label[:, None] == ext_label[None, :]) & ext_inside[None, :]
        scores = jnp.einsum('iphd,jphd->phij', q_own, k_ext) * scaling
        scores = jnp.where(allowed, scores, masked_score)
        row_max = lax.optimization_barrier(jnp.max(scores, axis=-1))
        log_total = row_max + jnp.log(lax.optimization_barrier(jnp.sum(jnp.exp(scores - row_max[..., None]), axis=-1)))
        weights = jnp.where(allowed, jnp.exp(scores - log_total[..., None]), 0.0)
        weights_low = rounded(weights)
        attended = jnp.einsum('phij,jphd->iphd', weights_low, v_ext)
        row_dot = jnp.einsum('iphd,iphd->phi', g_own, attended)
        weight_grad = jnp.einsum('iphd,jphd->phij', g_own, v_ext)
        score_grad = rounded(weights * (weight_grad - row_dot[..., None]))
        grad_query = jnp.einsum('phij,jphd->iphd', score_grad, k_ext) * scaling
        return (grad_query.reshape(WIN, S, HEADS * HDIM).astype(jnp.bfloat16), log_total, row_dot)
    groups = jnp.arange(N_GRP, dtype=jnp.int32)
    grad_q, log_totals, row_dots = lax.map(query_side, groups)

    def frame_major(stat):
        return jnp.pad(stat.transpose(0, 3, 1, 2).reshape(FRAMES, S, HEADS), margin)
    total_pad = frame_major(log_totals)
    dot_pad = frame_major(row_dots)

    def key_side(group_id):
        first_frame = group_id * WIN
        k_own = split_heads(lax.dynamic_slice_in_dim(k_time, first_frame, WIN, 0))
        v_own = split_heads(lax.dynamic_slice_in_dim(v_time, first_frame, WIN, 0))
        q_ext = split_heads(lax.dynamic_slice_in_dim(query_pad, first_frame, 3 * WIN, 0))
        g_ext = split_heads(lax.dynamic_slice_in_dim(cot_pad, first_frame, 3 * WIN, 0))
        total_ext = lax.dynamic_slice_in_dim(total_pad, first_frame, 3 * WIN, 0).transpose(1, 2, 0)
        dot_ext = lax.dynamic_slice_in_dim(dot_pad, first_frame, 3 * WIN, 0).transpose(1, 2, 0)
        own_label, own_inside = clip_labels(clip_len, first_frame, WIN, FRAMES)
        ext_label, ext_inside = clip_labels(clip_len, first_frame - WIN, 3 * WIN, FRAMES)
        allowed = ext_inside[:, None] & (ext_label[:, None] == own_label[None, :])
        scores = jnp.einsum('iphd,jphd->phij', q_ext, k_own) * scaling
        weights = jnp.where(allowed, jnp.exp(jnp.where(allowed, scores, masked_score) - total_ext[..., None]), 0.0)
        weights_low = rounded(weights)
        weight_grad = jnp.einsum('iphd,jphd->phij', g_ext, v_own)
        score_grad = rounded(weights * (weight_grad - dot_ext[..., None]))
        grad_key = jnp.einsum('phij,iphd->jphd', score_grad, q_ext) * scaling
        grad_value = jnp.einsum('phij,iphd->jphd', weights_low, g_ext)
        flat_shape = (WIN, S, HEADS * HDIM)
        return (grad_key.reshape(flat_shape).astype(jnp.bfloat16), grad_value.reshape(flat_shape).astype(jnp.bfloat16))
    grad_k, grad_v = lax.map(key_side, groups)
    full_shape = (FRAMES, S, HEADS * HDIM)
    return (grad_q.reshape(full_shape), grad_k.reshape(full_shape), grad_v.reshape(full_shape))

def reference(q_space, k_space, v_space, cot_space, q_time, k_time, v_time, cot_time, clip_len):
    grad_qs, grad_ks, grad_vs = lax.map(frame_grads, (q_space, k_space, v_space, cot_space))
    grad_qt, grad_kt, grad_vt = time_grads(q_time, k_time, v_time, cot_time, clip_len)
    return (grad_qs, grad_ks, grad_vs, grad_qt, grad_kt, grad_vt)
```

```python
import functools
import math

import jax
import jax.numpy as jnp
from jax import lax
from jax.experimental import pallas as pl
from jax.experimental.pallas import tpu as pltpu
from jax.sharding import PartitionSpec as P

HEADS = 8
HDIM = 72
LANES = 128
SCALE = 1.0 / math.sqrt(HDIM)
MASKED = -1e30
MESH = pl.DeviceIdType.MESH
BF = jnp.bfloat16
F32 = jnp.float32


def space_head(h, qs, ks, vs, cs, gq, gk, gv):
    q, k, v, c = qs[h], ks[h], vs[h], cs[h]
    first = (((0,), (0,)), ((), ()))
    last = (((1,), (1,)), ((), ()))
    plain = (((1,), (0,)), ((), ()))
    scores = lax.dot_general(k, q, first, preferred_element_type=F32) * SCALE
    peak = jnp.max(scores, axis=0, keepdims=True)
    grown = jnp.exp(scores - peak)
    weights = grown * (1.0 / jnp.sum(grown, axis=0, keepdims=True))
    low = weights.astype(BF)
    dweights = lax.dot_general(v, c, first, preferred_element_type=F32)
    dot = jnp.sum(low.astype(F32) * dweights, axis=0, keepdims=True)
    dscores = (weights * (dweights - dot)).astype(BF)
    gq[h] = (lax.dot_general(k, dscores, plain, preferred_element_type=F32) * SCALE).astype(BF)
    gk[h] = (lax.dot_general(q, dscores, last, preferred_element_type=F32) * SCALE).astype(BF)
    gv[h] = lax.dot_general(c, low, last, preferred_element_type=F32).astype(BF)


def kernel(
    nz, ng,
    qs, ks, vs, cs, qt, kt, vt, ct, labels, side,
    gqs, gks, gvs, gqt, gkt, gvt,
    s1, s2, s3, r1, r2, r3, o1, o2, t1, t2,
    fq, fk, fv, fg, fw, fl, fd,
    in_send, in_recv, hop_send, hop_recv, out_send, out_recv, self_sem,
):
    g = lax.axis_index("grp")
    z = lax.axis_index("seq")
    before = lax.rem(g + ng - 1, ng)
    after = lax.rem(g + 1, ng)

    def partner(d):
        return lax.rem(z + d, nz)

    barrier = pltpu.get_barrier_semaphore()
    for d in range(1, nz):
        pl.semaphore_signal(barrier, inc=1, device_id=(g, partner(d)), device_id_type=MESH)
    pl.semaphore_signal(barrier, inc=1, device_id=(before, z), device_id_type=MESH)
    pl.semaphore_signal(barrier, inc=1, device_id=(after, z), device_id_type=MESH)

    halves = [slice(0, LANES), slice(LANES, 2 * LANES)]
    for h in range(HEADS):
        for half in range(2):
            p = 2 * h + half
            s1[p, 0:HDIM, :] = qt[h, :, halves[half]]
            s1[p, HDIM : 2 * HDIM, :] = kt[h, :, halves[half]]
    pl.semaphore_wait(barrier, nz - 1 + 2)

    order = []
    for d in range(1, nz // 2):
        order += [d, nz - d]
    order.append(nz // 2)

    def send(stage, src, dst, sems_out, sems_in, d):
        return pltpu.make_async_remote_copy(
            src_ref=src.at[partner(d)], dst_ref=dst.at[z],
            send_sem=sems_out.at[stage, d], recv_sem=sems_in.at[stage, d],
            device_id=(g, partner(d)), device_id_type=MESH,
        )

    def own(src, dst, i):
        return pltpu.make_async_copy(src.at[z], dst.at[z], self_sem.at[i])

    def hop(stage, ref):
        return [
            pltpu.make_async_remote_copy(
                src_ref=ref.at[1], dst_ref=ref.at[0], send_sem=hop_send.at[stage, 0],
                recv_sem=hop_recv.at[stage, 0], device_id=(after, z), device_id_type=MESH,
            ),
            pltpu.make_async_remote_copy(
                src_ref=ref.at[1], dst_ref=ref.at[2], send_sem=hop_send.at[stage, 1],
                recv_sem=hop_recv.at[stage, 1], device_id=(before, z), device_id_type=MESH,
            ),
        ]

    firsts = [send(0, s1, r1.at[1], in_send, in_recv, d) for d in order]
    firsts.append(own(s1, r1.at[1], 0))
    for c in firsts:
        c.start()
    for h in range(HEADS):
        for half in range(2):
            p = 2 * h + half
            s2[p, 0:HDIM, :] = ct[h, :, halves[half]]
            s2[p, HDIM:, :] = vt[h, 0:8, halves[half]]
            s3[p] = vt[h, 8:, halves[half]]

    @pl.loop(0, HEADS)
    def _(h):
        space_head(h, qs, ks, vs, cs, gqs, gks, gvs)

    seconds = [send(1, s2, r2.at[1], in_send, in_recv, d) for d in order]
    seconds.append(own(s2, r2.at[1], 1))
    for c in seconds:
        c.start()
    for c in firsts:
        c.wait()
    hop1 = hop(0, r1)
    for c in hop1:
        c.start()
    thirds = [send(2, s3, r3.at[1], in_send, in_recv, d) for d in order]
    thirds.append(own(s3, r3.at[1], 2))
    for c in thirds:
        c.start()

    def lay(n, target, row, ref, low, high, at):
        count = high - low
        mine = ref[1, row, low:high, :].astype(F32)
        if n == 1:
            target[1, row, at : at + count, :] = mine
        else:
            other = ref[n, row, low:high, :].astype(F32)
            keep = side[n, row] > 0.5
            target[n, row, at : at + count, :] = jnp.where(keep[0:1, :], mine, other)

    def scores_of(n):
        label = labels[n]
        @pl.loop(0, nz)
        def _(i):
            s = jnp.sum(fq[n, i][None] * fk[n], axis=1) * SCALE
            same = label == labels[n, pl.ds(i, 1), :]
            s = jnp.where(same, s, MASKED)
            e = jnp.where(same, jnp.exp(s - jnp.max(s, axis=0, keepdims=True)), 0.0)
            w = e * (1.0 / jnp.sum(e, axis=0, keepdims=True))
            low = w.astype(BF).astype(F32)
            fw[n, i] = w
            fl[n, i] = jnp.broadcast_to(low[:, None, :], (nz, 8, LANES))

    def sum_over(rows, coef):
        acc = jnp.zeros((HDIM // 8, 8, LANES), F32)
        for m in range(nz):
            acc = acc + rows(m).reshape(HDIM // 8, 8, LANES) * coef(m)[None]
        return acc.reshape(HDIM, LANES)

    @pl.loop(0, nz)
    def _(i):
        lay(1, fq, i, r1, 0, HDIM, 0)
        lay(1, fk, i, r1, HDIM, 2 * HDIM, 0)

    scores_of(1)
    for c in hop1:
        c.wait()

    @pl.loop(0, nz)
    def _(i):
        for n in (0, 2):
            lay(n, fq, i, r1, 0, HDIM, 0)
            lay(n, fk, i, r1, HDIM, 2 * HDIM, 0)

    scores_of(0)
    scores_of(2)

    for c in seconds:
        c.wait()
    hop2 = hop(1, r2)
    for c in hop2:
        c.start()
    for c in hop2:
        c.wait()

    @pl.loop(0, nz)
    def _(i):
        for n in range(3):
            lay(n, fg, i, r2, 0, HDIM, 0)

    def pick(j, a, b, c):
        left = side[0, j, 0:1, :] > 0.5
        right = side[2, j, 0:1, :] > 0.5
        return jnp.where(left, a, jnp.where(right, c, b))

    @pl.loop(0, nz)
    def _(j):
        parts = [sum_over(lambda i: fg[n, i], lambda i: fl[n, i, j]) for n in range(3)]
        o1[j, 0:HDIM, :] = pick(j, *parts).astype(BF)
        o1[j, HDIM:, :] = jnp.zeros((8, LANES), BF)

    for c in thirds:
        c.wait()
    hop3 = hop(2, r3)
    for c in hop3:
        c.start()
    vouts = [send(0, o1, t1, out_send, out_recv, d) for d in order]
    vouts.append(own(o1, t1, 3))
    for c in vouts:
        c.start()
    for c in hop3:
        c.wait()

    @pl.loop(0, nz)
    def _(i):
        for n in range(3):
            lay(n, fv, i, r2, HDIM, HDIM + 8, 0)
            lay(n, fv, i, r3, 0, HDIM - 8, 8)

    @pl.loop(0, nz)
    def _(i):
        for n in range(3):
            dw = jnp.sum(fg[n, i][None] * fv[n], axis=1)
            w = fw[n, i]
            low = w.astype(BF).astype(F32)
            dot = jnp.sum(low * dw, axis=0, keepdims=True)
            ds = (w * (dw - dot)).astype(BF).astype(F32)
            fd[n, i] = jnp.broadcast_to(ds[:, None, :], (nz, 8, LANES))

    @pl.loop(0, nz)
    def _(i):
        parts = [sum_over(lambda j: fk[n, j], lambda j: fd[n, i, j]) for n in range(3)]
        o2[i, 0:HDIM, :] = (pick(i, *parts) * SCALE).astype(BF)
        parts = [sum_over(lambda j: fq[n, j], lambda j: fd[n, j, i]) for n in range(3)]
        o2[i, HDIM:, :] = (pick(i, *parts) * SCALE).astype(BF)

    qkouts = [send(1, o2, t2, out_send, out_recv, d) for d in order]
    qkouts.append(own(o2, t2, 4))
    for c in qkouts:
        c.start()
    for c in vouts:
        c.wait()
    for h in range(HEADS):
        for half in range(2):
            gvt[h, :, halves[half]] = t1[2 * h + half, 0:HDIM, :]
    for c in qkouts:
        c.wait()
    for h in range(HEADS):
        for half in range(2):
            gqt[h, :, halves[half]] = t2[2 * h + half, 0:HDIM, :]
            gkt[h, :, halves[half]] = t2[2 * h + half, HDIM:, :]


def clip_sides(clip_len, nz, ng):
    g = lax.axis_index("grp")
    first = g * nz
    ids = first - nz + jnp.arange(3 * nz, dtype=jnp.int32)
    ends = jnp.cumsum(clip_len)
    label = jnp.sum((ends[None, :] <= ids[:, None]).astype(jnp.int32), axis=1)
    label = jnp.where((ids >= 0) & (ids < nz * ng), label, -1)
    own = label[nz : 2 * nz]
    left = own == label[nz - 1]
    right = own == label[2 * nz]
    lab = jnp.stack(
        [jnp.where(left, own, label[:nz]), own, jnp.where(right, own, label[2 * nz :])]
    )
    side = jnp.stack([left, jnp.ones_like(left), right])
    lab = jnp.broadcast_to(lab.astype(F32)[:, :, None], (3, nz, LANES))
    side = jnp.broadcast_to(side.astype(F32)[:, :, None, None], (3, nz, 8, LANES))
    return lab, side


def solution(mesh):
    nz, ng = mesh.shape["seq"], mesh.shape["grp"]

    def shards(*args):
        clip_len = args[8]
        _, tokens, channels = args[0].shape
        flat = [jnp.swapaxes(a[0], 0, 1).reshape(HEADS, HDIM, tokens) for a in args[:8]]
        lab, side = clip_sides(clip_len, nz, ng)
        vmem = pl.BlockSpec(memory_space=pltpu.VMEM)
        dma = pltpu.SemaphoreType.DMA
        res = pl.pallas_call(
            functools.partial(kernel, nz, ng),
            out_shape=[jax.ShapeDtypeStruct((HEADS, HDIM, tokens), BF)] * 6,
            in_specs=[vmem] * 10,
            out_specs=[vmem] * 6,
            scratch_shapes=[
                pltpu.VMEM((nz, 2 * HDIM, LANES), BF),
                pltpu.VMEM((nz, HDIM + 8, LANES), BF),
                pltpu.VMEM((nz, HDIM - 8, LANES), BF),
                pltpu.VMEM((3, nz, 2 * HDIM, LANES), BF),
                pltpu.VMEM((3, nz, HDIM + 8, LANES), BF),
                pltpu.VMEM((3, nz, HDIM - 8, LANES), BF),
                pltpu.VMEM((nz, HDIM + 8, LANES), BF),
                pltpu.VMEM((nz, 2 * HDIM, LANES), BF),
                pltpu.VMEM((nz, HDIM + 8, LANES), BF),
                pltpu.VMEM((nz, 2 * HDIM, LANES), BF),
                pltpu.VMEM((3, nz, HDIM, LANES), F32),
                pltpu.VMEM((3, nz, HDIM, LANES), F32),
                pltpu.VMEM((3, nz, HDIM, LANES), F32),
                pltpu.VMEM((3, nz, HDIM, LANES), F32),
                pltpu.VMEM((3, nz, nz, LANES), F32),
                pltpu.VMEM((3, nz, nz, 8, LANES), F32),
                pltpu.VMEM((3, nz, nz, 8, LANES), F32),
                dma((3, nz)), dma((3, nz)), dma((3, 2)), dma((3, 2)), dma((2, nz)), dma((2, nz)),
                dma((5,)),
            ],
            compiler_params=pltpu.CompilerParams(
                collective_id=0, has_side_effects=True, vmem_limit_bytes=48 << 20
            ),
        )(*flat, lab, side)
        return tuple(jnp.swapaxes(r.reshape(channels, tokens), 0, 1)[None] for r in res)

    cut = P(("grp", "seq"), None, None)
    return jax.shard_map(
        shards, mesh=mesh, in_specs=(cut,) * 8 + (P(),), out_specs=(cut,) * 6, check_vma=False
    )
```

```python
import functools
import math

import jax
import jax.numpy as jnp
from jax import lax
from jax.experimental import pallas as pl
from jax.experimental.pallas import tpu as pltpu
from jax.sharding import PartitionSpec as P

HEADS = 8
HDIM = 72
LANES = 128
SCALE = 1.0 / math.sqrt(HDIM)
MASKED = -1e30
MESH = pl.DeviceIdType.MESH
REACHES = ((2, 0), (4, 2), (6, 2), (8, 2))
REACH = REACHES[0][0]
BF = jnp.bfloat16
F32 = jnp.float32


def space_head(h, qs, ks, vs, cs, gq, gk, gv):
    q, k, v, c = qs[h], ks[h], vs[h], cs[h]
    first = (((0,), (0,)), ((), ()))
    last = (((1,), (1,)), ((), ()))
    plain = (((1,), (0,)), ((), ()))
    scores = lax.dot_general(k, q, first, preferred_element_type=F32) * SCALE
    peak = jnp.max(scores, axis=0, keepdims=True)
    grown = jnp.exp(scores - peak)
    weights = grown * (1.0 / jnp.sum(grown, axis=0, keepdims=True))
    low = weights.astype(BF)
    dweights = lax.dot_general(v, c, first, preferred_element_type=F32)
    dot = jnp.sum(low.astype(F32) * dweights, axis=0, keepdims=True)
    dscores = (weights * (dweights - dot)).astype(BF)
    gq[h] = (lax.dot_general(k, dscores, plain, preferred_element_type=F32) * SCALE).astype(BF)
    gk[h] = (lax.dot_general(q, dscores, last, preferred_element_type=F32) * SCALE).astype(BF)
    gv[h] = lax.dot_general(c, low, last, preferred_element_type=F32).astype(BF)


def labels_of(clip_len, label, pick, nz, ng):
    g = lax.axis_index("grp")
    shape = (nz, LANES)
    slot = lax.broadcasted_iota(jnp.int32, shape, 0)
    ids = [slot + (g - 1 + n) * nz for n in range(3)]

    def count(c, carry):
        end, found = carry
        end = end + clip_len[c]
        return end, tuple(f + jnp.where(i >= end, 1, 0) for f, i in zip(found, ids))

    zero = jnp.zeros(shape, jnp.int32)
    _, found = lax.fori_loop(0, clip_len.shape[0], count, (jnp.int32(0), (zero,) * 3))
    low, own, high = [
        jnp.where((i >= 0) & (i < nz * ng), f, -1) for f, i in zip(found, ids)
    ]
    left = own == jnp.broadcast_to(low[nz - 1 : nz], shape)
    right = own == jnp.broadcast_to(high[0:1], shape)
    label[0] = jnp.where(left, own, low).astype(F32)
    label[1] = own.astype(F32)
    label[2] = jnp.where(right, own, high).astype(F32)
    for n, flag in ((0, left), (1, right)):
        pick[n] = jnp.broadcast_to(jnp.where(flag, 1.0, 0.0)[:, None, :], (nz, 8, LANES))


def kernel(
    nz, ng,
    clip_len, qs, ks, vs, cs, qt, kt, vt, ct,
    gqs, gks, gvs, gqt, gkt, gvt,
    iqs, iks, ivs, ics,
    r1, r2, r3, o1, o2,
    fq, fk, fv, fg, fw, fl, fd, labels, pick,
    bring, in_send, in_recv, hop_send, hop_recv, out_send, out_recv, self_sem, leave,
    right_in, left_in,
):
    g = lax.axis_index("grp")
    z = lax.axis_index("seq")
    before = lax.rem(g + ng - 1, ng)
    after = lax.rem(g + 1, ng)

    def partner(d):
        return lax.rem(z + d, nz)

    def tell(sem, group, place):
        pl.semaphore_signal(sem, inc=1, device_id=(group, place), device_id_type=MESH)

    def part(ref, p):
        half = p // HEADS
        lanes = pl.ds(pl.multiple_of(half * LANES, LANES), LANES)
        return ref.at[p - half * HEADS, :, lanes]

    def send(stage, src, dst, sems_out, sems_in, d):
        return pltpu.make_async_remote_copy(
            src_ref=src, dst_ref=dst, send_sem=sems_out.at[stage, d],
            recv_sem=sems_in.at[stage, d], device_id=(g, partner(d)), device_id_type=MESH,
        )

    def bring_in(stage, ref, dst, d):
        return send(stage, part(ref, partner(d)), dst, in_send, in_recv, d)

    def keep(src, dst, i):
        return pltpu.make_async_copy(src, dst, self_sem.at[i])

    def hop(stage, ref):
        return [
            pltpu.make_async_remote_copy(
                src_ref=ref.at[1], dst_ref=ref.at[0], send_sem=hop_send.at[stage, 0],
                recv_sem=hop_recv.at[stage, 0], device_id=(after, z), device_id_type=MESH,
            ),
            pltpu.make_async_remote_copy(
                src_ref=ref.at[1], dst_ref=ref.at[2], send_sem=hop_send.at[stage, 1],
                recv_sem=hop_recv.at[stage, 1], device_id=(before, z), device_id_type=MESH,
            ),
        ]

    order = [nz // 2]
    for d in range(nz // 2 - 1, 0, -1):
        order += [d, nz - d]

    barrier = pltpu.get_barrier_semaphore()
    for d in range(REACH, 0, -1):
        tell(barrier, g, partner(d))
        tell(barrier, g, partner(nz - d))
    tell(barrier, before, z)
    tell(barrier, after, z)
    pairs = ((qs, iqs), (ks, iks), (vs, ivs), (cs, ics))
    brought = [pltpu.make_async_copy(a, b, bring.at[i]) for i, (a, b) in enumerate(pairs)]
    for c in brought:
        c.start()
    firsts = [keep(part(qt, z), r1.at[1, z, 0], 0), keep(part(kt, z), r1.at[1, z, 1], 1)]
    for c in firsts:
        c.start()
    pl.semaphore_wait(barrier, 2 * REACH + 2)

    known, rounds = 0, 0
    for limit, step in REACHES:
        if known:
            for way, far in ((right_in, nz - step), (left_in, step)):
                tell(way.at[rounds], g, partner(far))
            pl.semaphore_wait(right_in.at[rounds], 1)
            pl.semaphore_wait(left_in.at[rounds], 1)
            rounds += 1
        for k in range(known + 1, limit + 1):
            for d in (k, nz - k) if k < nz - k else (k,):
                for which, ref in ((0, qt), (1, kt)):
                    copy = bring_in(which, ref, r1.at[1, z, which], d)
                    copy.start()
                    firsts.append(copy)
        known = limit
    for c in brought:
        c.wait()

    @pl.loop(0, HEADS)
    def _(h):
        space_head(h, iqs, iks, ivs, ics, iqs, iks, ivs)

    seconds = [keep(part(ct, z), r2.at[1, z], 2)]
    seconds += [bring_in(2, ct, r2.at[1, z], d) for d in order]
    for c in seconds:
        c.start()
    leaving = [
        pltpu.make_async_copy(a, b, leave.at[i])
        for i, (a, b) in enumerate(((iqs, gqs), (iks, gks), (ivs, gvs)))
    ]
    for c in leaving:
        c.start()
    labels_of(clip_len, labels, pick, nz, ng)
    for c in firsts:
        c.wait()
    hop1 = hop(0, r1)
    for c in hop1:
        c.start()
    thirds = [keep(part(vt, z), r3.at[1, z], 3)]
    thirds += [bring_in(3, vt, r3.at[1, z], d) for d in order]
    for c in thirds:
        c.start()

    def lay(n, target, row, ref, *which):
        mine = ref[(1, row) + which].astype(F32)
        if n == 1:
            target[1, row] = mine
        else:
            other = ref[(n, row) + which].astype(F32)
            target[n, row] = jnp.where(pick[n // 2, row, 0:1, :] > 0.5, mine, other)

    def scores_of(n):
        label = labels[n]

        @pl.loop(0, nz)
        def _(i):
            s = jnp.sum(fq[n, i][None] * fk[n], axis=1) * SCALE
            same = label == labels[n, pl.ds(i, 1), :]
            s = jnp.where(same, s, MASKED)
            e = jnp.where(same, jnp.exp(s - jnp.max(s, axis=0, keepdims=True)), 0.0)
            w = e * (1.0 / jnp.sum(e, axis=0, keepdims=True))
            low = w.astype(BF).astype(F32)
            fw[n, i] = w
            fl[n, i] = jnp.broadcast_to(low[:, None, :], (nz, 8, LANES))

    def sum_over(rows, coef):
        acc = jnp.zeros((HDIM // 8, 8, LANES), F32)
        for m in range(nz):
            acc = acc + rows(m).reshape(HDIM // 8, 8, LANES) * coef(m)[None]
        return acc.reshape(HDIM, LANES)

    @pl.loop(0, nz)
    def _(i):
        lay(1, fq, i, r1, 0)
        lay(1, fk, i, r1, 1)

    scores_of(1)
    for c in hop1:
        c.wait()

    @pl.loop(0, nz)
    def _(i):
        for n in (0, 2):
            lay(n, fq, i, r1, 0)
            lay(n, fk, i, r1, 1)

    scores_of(0)
    scores_of(2)

    for c in seconds:
        c.wait()
    hop2 = hop(1, r2)
    for c in hop2:
        c.start()

    @pl.loop(0, nz)
    def _(i):
        lay(1, fg, i, r2)

    for c in hop2:
        c.wait()

    @pl.loop(0, nz)
    def _(i):
        for n in (0, 2):
            lay(n, fg, i, r2)

    def choose(j, a, b, c):
        left = pick[0, j, 0:1, :] > 0.5
        right = pick[1, j, 0:1, :] > 0.5
        return jnp.where(left, a, jnp.where(right, c, b))

    def value_grad(j):
        parts = [sum_over(lambda i: fg[n, i], lambda i: fl[n, i, j]) for n in range(3)]
        o1[j] = choose(j, *parts).astype(BF)

    def query_key_grads(i):
        parts = [sum_over(lambda j: fk[n, j], lambda j: fd[n, i, j]) for n in range(3)]
        o2[0, i] = (choose(i, *parts) * SCALE).astype(BF)
        parts = [sum_over(lambda j: fq[n, j], lambda j: fd[n, j, i]) for n in range(3)]
        o2[1, i] = (choose(i, *parts) * SCALE).astype(BF)

    def return_all(make, ways):
        def back(stage, src, dst, d):
            return send(stage, src.at[partner(d)], part(dst, z), out_send, out_recv, d)

        @pl.loop(0, nz - 1)
        def _(step):
            far = nz // 2 - (step + 1) // 2
            odd = lax.rem(step, 2)
            d = far * odd + (nz - far) * (1 - odd)
            make(partner(d))
            for stage, src, dst in ways:
                back(stage, src, dst, d).start()

        make(z)
        mine = [keep(src.at[z], part(dst, z), 4 + stage) for stage, src, dst in ways]
        for c in mine:
            c.start()
        return [back(stage, src, dst, d) for stage, src, dst in ways for d in order] + mine

    vouts = return_all(value_grad, [(0, o1, gvt)])

    for c in thirds:
        c.wait()
    hop3 = hop(2, r3)
    for c in hop3:
        c.start()

    def score_grads(n):
        @pl.loop(0, nz)
        def _(i):
            lay(n, fv, i, r3)

        @pl.loop(0, nz)
        def _(i):
            dw = jnp.sum(fg[n, i][None] * fv[n], axis=1)
            w = fw[n, i]
            low = w.astype(BF).astype(F32)
            dot = jnp.sum(low * dw, axis=0, keepdims=True)
            ds = (w * (dw - dot)).astype(BF).astype(F32)
            fd[n, i] = jnp.broadcast_to(ds[:, None, :], (nz, 8, LANES))

    score_grads(1)
    for c in hop3:
        c.wait()
    score_grads(0)
    score_grads(2)

    qkouts = return_all(query_key_grads, [(1, o2.at[0], gqt), (2, o2.at[1], gkt)])
    for c in vouts + qkouts + leaving:
        c.wait()


def hand_over(*refs):
    ins, outs, held, sems = refs[:6], refs[6:12], refs[12:18], refs[18]
    pulls = [pltpu.make_async_copy(a, b, sems.at[0, i]) for i, (a, b) in enumerate(zip(ins, held))]
    pushes = [pltpu.make_async_copy(a, b, sems.at[1, i]) for i, (a, b) in enumerate(zip(held, outs))]
    for c in pulls:
        c.start()
    for c, d in zip(pulls, pushes):
        c.wait()
        d.start()
    for c in pushes:
        c.wait()


def solution(mesh):
    nz, ng = mesh.shape["seq"], mesh.shape["grp"]

    def shards(*args):
        clip_len = args[8]
        _, tokens, channels = args[0].shape
        flat = [jnp.swapaxes(a[0], 0, 1).reshape(HEADS, HDIM, tokens) for a in args[:8]]
        anywhere = pl.BlockSpec(memory_space=pl.ANY)
        dma = pltpu.SemaphoreType.DMA
        frame = (HEADS, HDIM, tokens)
        outs = [jax.ShapeDtypeStruct(frame, BF)] * 6
        res = pl.pallas_call(
            functools.partial(kernel, nz, ng),
            out_shape=outs,
            in_specs=[pl.BlockSpec(memory_space=pltpu.SMEM)] + [anywhere] * 8,
            out_specs=[anywhere] * 6,
            scratch_shapes=[pltpu.VMEM(frame, BF)] * 4
            + [
                pltpu.VMEM((3, nz, 2, HDIM, LANES), BF),
                pltpu.VMEM((3, nz, HDIM, LANES), BF),
                pltpu.VMEM((3, nz, HDIM, LANES), BF),
                pltpu.VMEM((nz, HDIM, LANES), BF),
                pltpu.VMEM((2, nz, HDIM, LANES), BF),
                pltpu.VMEM((3, nz, HDIM, LANES), F32),
                pltpu.VMEM((3, nz, HDIM, LANES), F32),
                pltpu.VMEM((3, nz, HDIM, LANES), F32),
                pltpu.VMEM((3, nz, HDIM, LANES), F32),
                pltpu.VMEM((3, nz, nz, LANES), F32),
                pltpu.VMEM((3, nz, nz, 8, LANES), F32),
                pltpu.VMEM((3, nz, nz, 8, LANES), F32),
                pltpu.VMEM((3, nz, LANES), F32),
                pltpu.VMEM((2, nz, 8, LANES), F32),
                dma((4,)), dma((4, nz)), dma((4, nz)), dma((3, 2)), dma((3, 2)),
                dma((3, nz)), dma((3, nz)), dma((7,)), dma((3,)),
                pltpu.SemaphoreType.REGULAR((len(REACHES) - 1,)),
                pltpu.SemaphoreType.REGULAR((len(REACHES) - 1,)),
            ],
            compiler_params=pltpu.CompilerParams(
                collective_id=0, has_side_effects=True, vmem_limit_bytes=63 << 20
            ),
        )(clip_len, *flat)
        res = pl.pallas_call(
            hand_over,
            out_shape=outs,
            in_specs=[anywhere] * 6,
            out_specs=[anywhere] * 6,
            scratch_shapes=[pltpu.VMEM(frame, BF)] * 6 + [dma((2, 6))],
            compiler_params=pltpu.CompilerParams(vmem_limit_bytes=63 << 20),
        )(*res)
        return tuple(jnp.swapaxes(r.reshape(channels, tokens), 0, 1)[None] for r in res)

    cut = P(("grp", "seq"), None, None)
    return jax.shard_map(
        shards, mesh=mesh, in_specs=(cut,) * 8 + (P(),), out_specs=(cut,) * 6, check_vma=False
    )
```

```python
import functools
import math

import jax
import jax.numpy as jnp
from jax import lax
from jax.experimental import pallas as pl
from jax.experimental.pallas import tpu as pltpu
from jax.sharding import PartitionSpec as P

HEADS = 8
HDIM = 72
LANES = 128
SCALE = 1.0 / math.sqrt(HDIM)
MASKED = -1e30
MESH = pl.DeviceIdType.MESH
REACHES = ((2, 0), (4, 2), (6, 2), (8, 2))
REACH = REACHES[0][0]
BF = jnp.bfloat16
F32 = jnp.float32


def space_head(h, qs, ks, vs, cs, gq, gk, gv):
    q, k, v, c = qs[h], ks[h], vs[h], cs[h]
    first = (((0,), (0,)), ((), ()))
    last = (((1,), (1,)), ((), ()))
    plain = (((1,), (0,)), ((), ()))
    scores = lax.dot_general(k, q, first, preferred_element_type=F32) * SCALE
    peak = jnp.max(scores, axis=0, keepdims=True)
    grown = jnp.exp(scores - peak)
    weights = grown * (1.0 / jnp.sum(grown, axis=0, keepdims=True))
    low = weights.astype(BF)
    dweights = lax.dot_general(v, c, first, preferred_element_type=F32)
    dot = jnp.sum(low.astype(F32) * dweights, axis=0, keepdims=True)
    dscores = (weights * (dweights - dot)).astype(BF)
    gq[h] = (lax.dot_general(k, dscores, plain, preferred_element_type=F32) * SCALE).astype(BF)
    gk[h] = (lax.dot_general(q, dscores, last, preferred_element_type=F32) * SCALE).astype(BF)
    gv[h] = lax.dot_general(c, low, last, preferred_element_type=F32).astype(BF)


def labels_of(clip_len, label, pick, nz, ng):
    g = lax.axis_index("grp")
    shape = (nz, LANES)
    slot = lax.broadcasted_iota(jnp.int32, shape, 0)
    ids = [slot + (g - 1 + n) * nz for n in range(3)]

    def count(c, carry):
        end, found = carry
        end = end + clip_len[c]
        return end, tuple(f + jnp.where(i >= end, 1, 0) for f, i in zip(found, ids))

    zero = jnp.zeros(shape, jnp.int32)
    _, found = lax.fori_loop(0, clip_len.shape[0], count, (jnp.int32(0), (zero,) * 3))
    low, own, high = [
        jnp.where((i >= 0) & (i < nz * ng), f, -1) for f, i in zip(found, ids)
    ]
    left = own == jnp.broadcast_to(low[nz - 1 : nz], shape)
    right = own == jnp.broadcast_to(high[0:1], shape)
    label[0] = jnp.where(left, own, low).astype(F32)
    label[1] = own.astype(F32)
    label[2] = jnp.where(right, own, high).astype(F32)
    for n, flag in ((0, left), (1, right)):
        pick[n] = jnp.broadcast_to(jnp.where(flag, 1.0, 0.0)[:, None, :], (nz, 8, LANES))


def kernel(
    nz, ng,
    clip_len, qs, ks, vs, cs, qt, kt, vt, ct,
    gqs, gks, gvs, gqt, gkt, gvt,
    iqs, iks, ivs, ics,
    r1, r2, r3, o1, o2,
    fq, fk, fv, fg, fw, fl, fd, labels, pick,
    bring, in_send, in_recv, hop_send, hop_recv, out_send, out_recv, self_sem, leave,
    right_in, left_in,
):
    g = lax.axis_index("grp")
    z = lax.axis_index("seq")
    before = lax.rem(g + ng - 1, ng)
    after = lax.rem(g + 1, ng)

    def partner(d):
        return lax.rem(z + d, nz)

    def tell(sem, group, place):
        pl.semaphore_signal(sem, inc=1, device_id=(group, place), device_id_type=MESH)

    def part(ref, p):
        half = p // HEADS
        lanes = pl.ds(pl.multiple_of(half * LANES, LANES), LANES)
        return ref.at[p - half * HEADS, :, lanes]

    def send(stage, src, dst, sems_out, sems_in, d):
        return pltpu.make_async_remote_copy(
            src_ref=src, dst_ref=dst, send_sem=sems_out.at[stage, d],
            recv_sem=sems_in.at[stage, d], device_id=(g, partner(d)), device_id_type=MESH,
        )

    def bring_in(stage, ref, dst, d):
        return send(stage, part(ref, partner(d)), dst, in_send, in_recv, d)

    def keep(src, dst, i):
        return pltpu.make_async_copy(src, dst, self_sem.at[i])

    def hop(stage, ref):
        return [
            pltpu.make_async_remote_copy(
                src_ref=ref.at[1], dst_ref=ref.at[0], send_sem=hop_send.at[stage, 0],
                recv_sem=hop_recv.at[stage, 0], device_id=(after, z), device_id_type=MESH,
            ),
            pltpu.make_async_remote_copy(
                src_ref=ref.at[1], dst_ref=ref.at[2], send_sem=hop_send.at[stage, 1],
                recv_sem=hop_recv.at[stage, 1], device_id=(before, z), device_id_type=MESH,
            ),
        ]

    order = [nz // 2]
    for d in range(nz // 2 - 1, 0, -1):
        order += [d, nz - d]

    barrier = pltpu.get_barrier_semaphore()
    for d in range(REACH, 0, -1):
        tell(barrier, g, partner(d))
        tell(barrier, g, partner(nz - d))
    tell(barrier, before, z)
    tell(barrier, after, z)
    pairs = ((qs, iqs), (ks, iks), (vs, ivs), (cs, ics))
    brought = [pltpu.make_async_copy(a, b, bring.at[i]) for i, (a, b) in enumerate(pairs)]
    for c in brought:
        c.start()
    firsts = [keep(part(qt, z), r1.at[1, z, 0], 0), keep(part(kt, z), r1.at[1, z, 1], 1)]
    for c in firsts:
        c.start()
    pl.semaphore_wait(barrier, 2 * REACH + 2)

    known, rounds = 0, 0
    for limit, step in REACHES:
        if known:
            for way, far in ((right_in, nz - step), (left_in, step)):
                tell(way.at[rounds], g, partner(far))
            pl.semaphore_wait(right_in.at[rounds], 1)
            pl.semaphore_wait(left_in.at[rounds], 1)
            rounds += 1
        for k in range(known + 1, limit + 1):
            for d in (k, nz - k) if k < nz - k else (k,):
                for which, ref in ((0, qt), (1, kt)):
                    copy = bring_in(which, ref, r1.at[1, z, which], d)
                    copy.start()
                    firsts.append(copy)
        known = limit
    for c in brought:
        c.wait()

    @pl.loop(0, HEADS)
    def _(h):
        space_head(h, iqs, iks, ivs, ics, iqs, iks, ivs)

    seconds = [keep(part(ct, z), r2.at[1, z], 2)]
    seconds += [bring_in(2, ct, r2.at[1, z], d) for d in order]
    for c in seconds:
        c.start()
    leaving = [
        pltpu.make_async_copy(a, b, leave.at[i])
        for i, (a, b) in enumerate(((iqs, gqs), (iks, gks), (ivs, gvs)))
    ]
    for c in leaving:
        c.start()
    labels_of(clip_len, labels, pick, nz, ng)
    for c in firsts:
        c.wait()
    hop1 = hop(0, r1)
    for c in hop1:
        c.start()
    thirds = [keep(part(vt, z), r3.at[1, z], 3)]
    thirds += [bring_in(3, vt, r3.at[1, z], d) for d in order]
    for c in thirds:
        c.start()

    def lay(n, target, row, ref, *which):
        mine = ref[(1, row) + which].astype(F32)
        if n == 1:
            target[1, row] = mine
        else:
            other = ref[(n, row) + which].astype(F32)
            target[n, row] = jnp.where(pick[n // 2, row, 0:1, :] > 0.5, mine, other)

    def scores_of(n):
        label = labels[n]

        @pl.loop(0, nz)
        def _(i):
            s = jnp.sum(fq[n, i][None] * fk[n], axis=1) * SCALE
            same = label == labels[n, pl.ds(i, 1), :]
            s = jnp.where(same, s, MASKED)
            e = jnp.where(same, jnp.exp(s - jnp.max(s, axis=0, keepdims=True)), 0.0)
            w = e * (1.0 / jnp.sum(e, axis=0, keepdims=True))
            low = w.astype(BF).astype(F32)
            fw[n, i] = w
            fl[n, i] = jnp.broadcast_to(low[:, None, :], (nz, 8, LANES))

    def sum_over(rows, coef):
        acc = jnp.zeros((HDIM // 8, 8, LANES), F32)
        for m in range(nz):
            acc = acc + rows(m).reshape(HDIM // 8, 8, LANES) * coef(m)[None]
        return acc.reshape(HDIM, LANES)

    @pl.loop(0, nz)
    def _(i):
        lay(1, fq, i, r1, 0)
        lay(1, fk, i, r1, 1)

    scores_of(1)
    for c in hop1:
        c.wait()

    for c in seconds:
        c.wait()
    hop2 = hop(1, r2)
    for c in hop2:
        c.start()

    @pl.loop(0, nz)
    def _(i):
        for n in (0, 2):
            lay(n, fq, i, r1, 0)
            lay(n, fk, i, r1, 1)

    scores_of(0)
    scores_of(2)

    @pl.loop(0, nz)
    def _(i):
        lay(1, fg, i, r2)

    for c in hop2:
        c.wait()

    @pl.loop(0, nz)
    def _(i):
        for n in (0, 2):
            lay(n, fg, i, r2)

    def choose(j, a, b, c):
        left = pick[0, j, 0:1, :] > 0.5
        right = pick[1, j, 0:1, :] > 0.5
        return jnp.where(left, a, jnp.where(right, c, b))

    def value_grad(j):
        parts = [sum_over(lambda i: fg[n, i], lambda i: fl[n, i, j]) for n in range(3)]
        o1[j] = choose(j, *parts).astype(BF)

    def return_all(make, ways):
        def back(stage, src, dst, d):
            return send(stage, src.at[partner(d)], part(dst, z), out_send, out_recv, d)

        @pl.loop(0, nz - 1)
        def _(step):
            far = nz // 2 - (step + 1) // 2
            odd = lax.rem(step, 2)
            d = far * odd + (nz - far) * (1 - odd)
            make(partner(d))
            for stage, src, dst in ways:
                back(stage, src, dst, d).start()

        make(z)
        mine = [keep(src.at[z], part(dst, z), 4 + stage) for stage, src, dst in ways]
        for c in mine:
            c.start()
        return [back(stage, src, dst, d) for stage, src, dst in ways for d in order] + mine

    vouts = return_all(value_grad, [(0, o1, gvt)])

    for c in thirds:
        c.wait()
    hop3 = hop(2, r3)
    for c in hop3:
        c.start()

    def lay_values(*sets):
        @pl.loop(0, nz)
        def _(i):
            for n in sets:
                lay(n, fv, i, r3)

    def score_grad_row(n, i):
        dw = jnp.sum(fg[n, i][None] * fv[n], axis=1)
        w = fw[n, i]
        low = w.astype(BF).astype(F32)
        dot = jnp.sum(low * dw, axis=0, keepdims=True)
        ds = (w * (dw - dot)).astype(BF).astype(F32)
        fd[n, i] = jnp.broadcast_to(ds[:, None, :], (nz, 8, LANES))

    lay_values(1)

    @pl.loop(0, nz)
    def _(i):
        score_grad_row(1, i)

    for c in hop3:
        c.wait()
    lay_values(0, 2)

    def query_grad(i):
        score_grad_row(0, i)
        score_grad_row(2, i)
        parts = [sum_over(lambda j: fk[n, j], lambda j: fd[n, i, j]) for n in range(3)]
        o2[0, i] = (choose(i, *parts) * SCALE).astype(BF)

    def key_grad(j):
        parts = [sum_over(lambda i: fq[n, i], lambda i: fd[n, i, j]) for n in range(3)]
        o2[1, j] = (choose(j, *parts) * SCALE).astype(BF)

    qkouts = return_all(query_grad, [(1, o2.at[0], gqt)])
    qkouts += return_all(key_grad, [(2, o2.at[1], gkt)])
    for c in vouts + qkouts + leaving:
        c.wait()


def hand_over(*refs):
    ins, outs, held, sems = refs[:6], refs[6:12], refs[12:18], refs[18]
    pulls = [pltpu.make_async_copy(a, b, sems.at[0, i]) for i, (a, b) in enumerate(zip(ins, held))]
    pushes = [pltpu.make_async_copy(a, b, sems.at[1, i]) for i, (a, b) in enumerate(zip(held, outs))]
    for c in pulls:
        c.start()
    for c, d in zip(pulls, pushes):
        c.wait()
        d.start()
    for c in pushes:
        c.wait()


def solution(mesh):
    nz, ng = mesh.shape["seq"], mesh.shape["grp"]

    def shards(*args):
        clip_len = args[8]
        _, tokens, channels = args[0].shape
        flat = [jnp.swapaxes(a[0], 0, 1).reshape(HEADS, HDIM, tokens) for a in args[:8]]
        anywhere = pl.BlockSpec(memory_space=pl.ANY)
        dma = pltpu.SemaphoreType.DMA
        frame = (HEADS, HDIM, tokens)
        outs = [jax.ShapeDtypeStruct(frame, BF)] * 6
        res = pl.pallas_call(
            functools.partial(kernel, nz, ng),
            out_shape=outs,
            in_specs=[pl.BlockSpec(memory_space=pltpu.SMEM)] + [anywhere] * 8,
            out_specs=[anywhere] * 6,
            scratch_shapes=[pltpu.VMEM(frame, BF)] * 4
            + [
                pltpu.VMEM((3, nz, 2, HDIM, LANES), BF),
                pltpu.VMEM((3, nz, HDIM, LANES), BF),
                pltpu.VMEM((3, nz, HDIM, LANES), BF),
                pltpu.VMEM((nz, HDIM, LANES), BF),
                pltpu.VMEM((2, nz, HDIM, LANES), BF),
                pltpu.VMEM((3, nz, HDIM, LANES), F32),
                pltpu.VMEM((3, nz, HDIM, LANES), F32),
                pltpu.VMEM((3, nz, HDIM, LANES), F32),
                pltpu.VMEM((3, nz, HDIM, LANES), F32),
                pltpu.VMEM((3, nz, nz, LANES), F32),
                pltpu.VMEM((3, nz, nz, 8, LANES), F32),
                pltpu.VMEM((3, nz, nz, 8, LANES), F32),
                pltpu.VMEM((3, nz, LANES), F32),
                pltpu.VMEM((2, nz, 8, LANES), F32),
                dma((4,)), dma((4, nz)), dma((4, nz)), dma((3, 2)), dma((3, 2)),
                dma((3, nz)), dma((3, nz)), dma((7,)), dma((3,)),
                pltpu.SemaphoreType.REGULAR((len(REACHES) - 1,)),
                pltpu.SemaphoreType.REGULAR((len(REACHES) - 1,)),
            ],
            compiler_params=pltpu.CompilerParams(
                collective_id=0, has_side_effects=True, vmem_limit_bytes=63 << 20
            ),
        )(clip_len, *flat)
        res = pl.pallas_call(
            hand_over,
            out_shape=outs,
            in_specs=[anywhere] * 6,
            out_specs=[anywhere] * 6,
            scratch_shapes=[pltpu.VMEM(frame, BF)] * 6 + [dma((2, 6))],
            compiler_params=pltpu.CompilerParams(vmem_limit_bytes=63 << 20),
        )(*res)
        return tuple(jnp.swapaxes(r.reshape(channels, tokens), 0, 1)[None] for r in res)

    cut = P(("grp", "seq"), None, None)
    return jax.shard_map(
        shards, mesh=mesh, in_specs=(cut,) * 8 + (P(),), out_specs=(cut,) * 6, check_vma=False
    )
```

```python
import functools
import math

import jax
import jax.numpy as jnp
from jax import lax
from jax.experimental import pallas as pl
from jax.experimental.pallas import tpu as pltpu
from jax.sharding import PartitionSpec as P

HEADS = 8
HDIM = 72
LANES = 128
SCALE = 1.0 / math.sqrt(HDIM)
MASKED = -1e30
MESH = pl.DeviceIdType.MESH
REACHES = ((2, 0), (4, 2), (6, 2), (8, 2))
REACH = REACHES[0][0]
BF = jnp.bfloat16
F32 = jnp.float32


def space_head(h, qs, ks, vs, cs, gq, gk, gv):
    q, k, v, c = qs[h], ks[h], vs[h], cs[h]
    first = (((0,), (0,)), ((), ()))
    last = (((1,), (1,)), ((), ()))
    plain = (((1,), (0,)), ((), ()))
    scores = lax.dot_general(k, q, first, preferred_element_type=F32) * SCALE
    peak = jnp.max(scores, axis=0, keepdims=True)
    grown = jnp.exp(scores - peak)
    weights = grown * (1.0 / jnp.sum(grown, axis=0, keepdims=True))
    low = weights.astype(BF)
    dweights = lax.dot_general(v, c, first, preferred_element_type=F32)
    dot = jnp.sum(low.astype(F32) * dweights, axis=0, keepdims=True)
    dscores = (weights * (dweights - dot)).astype(BF)
    gq[h] = (lax.dot_general(k, dscores, plain, preferred_element_type=F32) * SCALE).astype(BF)
    gk[h] = (lax.dot_general(q, dscores, last, preferred_element_type=F32) * SCALE).astype(BF)
    gv[h] = lax.dot_general(c, low, last, preferred_element_type=F32).astype(BF)


def labels_of(clip_len, label, pick, nz, ng):
    g = lax.axis_index("grp")
    shape = (nz, LANES)
    slot = lax.broadcasted_iota(jnp.int32, shape, 0)
    ids = [slot + (g - 1 + n) * nz for n in range(3)]

    def count(c, carry):
        end, found = carry
        end = end + clip_len[c]
        return end, tuple(f + jnp.where(i >= end, 1, 0) for f, i in zip(found, ids))

    zero = jnp.zeros(shape, jnp.int32)
    _, found = lax.fori_loop(0, clip_len.shape[0], count, (jnp.int32(0), (zero,) * 3))
    low, own, high = [
        jnp.where((i >= 0) & (i < nz * ng), f, -1) for f, i in zip(found, ids)
    ]
    left = own == jnp.broadcast_to(low[nz - 1 : nz], shape)
    right = own == jnp.broadcast_to(high[0:1], shape)
    label[0] = jnp.where(left, own, low).astype(F32)
    label[1] = own.astype(F32)
    label[2] = jnp.where(right, own, high).astype(F32)
    for n, flag in ((0, left), (1, right)):
        pick[n] = jnp.broadcast_to(jnp.where(flag, 1.0, 0.0)[:, None, :], (nz, 8, LANES))


def kernel(
    nz, ng,
    clip_src, qs, ks, vs, cs, qt, kt, vt, ct,
    gqs, gks, gvs, gqt, gkt, gvt,
    iqs, iks, ivs, ics,
    r1, r2, r3, o1, o2,
    fq, fk, fv, fg, fw, fl, fd, labels, pick,
    bring, in_send, in_recv, hop_send, hop_recv, out_send, out_recv, self_sem, leave,
    right_in, left_in, clip_len,
):
    g = lax.axis_index("grp")
    z = lax.axis_index("seq")
    before = lax.rem(g + ng - 1, ng)
    after = lax.rem(g + 1, ng)

    def partner(d):
        return lax.rem(z + d, nz)

    def tell(sem, group, place):
        pl.semaphore_signal(sem, inc=1, device_id=(group, place), device_id_type=MESH)

    def part(ref, p):
        half = p // HEADS
        lanes = pl.ds(pl.multiple_of(half * LANES, LANES), LANES)
        return ref.at[p - half * HEADS, :, lanes]

    def send(stage, src, dst, sems_out, sems_in, d):
        return pltpu.make_async_remote_copy(
            src_ref=src, dst_ref=dst, send_sem=sems_out.at[stage, d],
            recv_sem=sems_in.at[stage, d], device_id=(g, partner(d)), device_id_type=MESH,
        )

    def bring_in(stage, ref, dst, d):
        return send(stage, part(ref, partner(d)), dst, in_send, in_recv, d)

    def keep(src, dst, i):
        return pltpu.make_async_copy(src, dst, self_sem.at[i])

    def hop(stage, ref):
        return [
            pltpu.make_async_remote_copy(
                src_ref=ref.at[1], dst_ref=ref.at[0], send_sem=hop_send.at[stage, 0],
                recv_sem=hop_recv.at[stage, 0], device_id=(after, z), device_id_type=MESH,
            ),
            pltpu.make_async_remote_copy(
                src_ref=ref.at[1], dst_ref=ref.at[2], send_sem=hop_send.at[stage, 1],
                recv_sem=hop_recv.at[stage, 1], device_id=(before, z), device_id_type=MESH,
            ),
        ]

    order = [nz // 2]
    for d in range(nz // 2 - 1, 0, -1):
        order += [d, nz - d]

    barrier = pltpu.get_barrier_semaphore()
    for d in range(REACH, 0, -1):
        tell(barrier, g, partner(d))
        tell(barrier, g, partner(nz - d))
    tell(barrier, before, z)
    tell(barrier, after, z)
    pairs = ((qs, iqs), (ks, iks), (vs, ivs), (cs, ics), (clip_src, clip_len))
    brought = [pltpu.make_async_copy(a, b, bring.at[i]) for i, (a, b) in enumerate(pairs)]
    for c in brought:
        c.start()
    firsts = [keep(part(qt, z), r1.at[1, z, 0], 0), keep(part(kt, z), r1.at[1, z, 1], 1)]
    for c in firsts:
        c.start()
    pl.semaphore_wait(barrier, 2 * REACH + 2)

    known, rounds = 0, 0
    for limit, step in REACHES:
        if known:
            for way, far in ((right_in, nz - step), (left_in, step)):
                tell(way.at[rounds], g, partner(far))
            pl.semaphore_wait(right_in.at[rounds], 1)
            pl.semaphore_wait(left_in.at[rounds], 1)
            rounds += 1
        for k in range(known + 1, limit + 1):
            for d in (k, nz - k) if k < nz - k else (k,):
                for which, ref in ((0, qt), (1, kt)):
                    copy = bring_in(which, ref, r1.at[1, z, which], d)
                    copy.start()
                    firsts.append(copy)
        known = limit
    for c in brought:
        c.wait()

    @pl.loop(0, HEADS)
    def _(h):
        space_head(h, iqs, iks, ivs, ics, iqs, iks, ivs)

    seconds = [keep(part(ct, z), r2.at[1, z], 2)]
    seconds += [bring_in(2, ct, r2.at[1, z], d) for d in order]
    for c in seconds:
        c.start()
    leaving = [
        pltpu.make_async_copy(a, b, leave.at[i])
        for i, (a, b) in enumerate(((iqs, gqs), (iks, gks), (ivs, gvs)))
    ]
    for c in leaving:
        c.start()
    labels_of(clip_len, labels, pick, nz, ng)
    for c in firsts:
        c.wait()
    hop1 = hop(0, r1)
    for c in hop1:
        c.start()
    thirds = [keep(part(vt, z), r3.at[1, z], 3)]
    thirds += [bring_in(3, vt, r3.at[1, z], d) for d in order]
    for c in thirds:
        c.start()

    def lay(n, target, row, ref, *which):
        mine = ref[(1, row) + which].astype(F32)
        if n == 1:
            target[1, row] = mine
        else:
            other = ref[(n, row) + which].astype(F32)
            target[n, row] = jnp.where(pick[n // 2, row, 0:1, :] > 0.5, mine, other)

    def scores_of(n):
        label = labels[n]

        @pl.loop(0, nz)
        def _(i):
            s = jnp.sum(fq[n, i][None] * fk[n], axis=1) * SCALE
            same = label == labels[n, pl.ds(i, 1), :]
            s = jnp.where(same, s, MASKED)
            e = jnp.where(same, jnp.exp(s - jnp.max(s, axis=0, keepdims=True)), 0.0)
            w = e * (1.0 / jnp.sum(e, axis=0, keepdims=True))
            low = w.astype(BF).astype(F32)
            fw[n, i] = w
            fl[n, i] = jnp.broadcast_to(low[:, None, :], (nz, 8, LANES))

    def sum_over(rows, coef):
        acc = jnp.zeros((HDIM // 8, 8, LANES), F32)
        for m in range(nz):
            acc = acc + rows(m).reshape(HDIM // 8, 8, LANES) * coef(m)[None]
        return acc.reshape(HDIM, LANES)

    @pl.loop(0, nz)
    def _(i):
        lay(1, fq, i, r1, 0)
        lay(1, fk, i, r1, 1)

    scores_of(1)
    for c in hop1:
        c.wait()

    for c in seconds:
        c.wait()
    hop2 = hop(1, r2)
    for c in hop2:
        c.start()

    @pl.loop(0, nz)
    def _(i):
        for n in (0, 2):
            lay(n, fq, i, r1, 0)
            lay(n, fk, i, r1, 1)

    scores_of(0)
    scores_of(2)

    @pl.loop(0, nz)
    def _(i):
        lay(1, fg, i, r2)

    for c in hop2:
        c.wait()

    @pl.loop(0, nz)
    def _(i):
        for n in (0, 2):
            lay(n, fg, i, r2)

    def choose(j, a, b, c):
        left = pick[0, j, 0:1, :] > 0.5
        right = pick[1, j, 0:1, :] > 0.5
        return jnp.where(left, a, jnp.where(right, c, b))

    def value_grad(j):
        parts = [sum_over(lambda i: fg[n, i], lambda i: fl[n, i, j]) for n in range(3)]
        o1[j] = choose(j, *parts).astype(BF)

    def return_all(make, ways):
        def back(stage, src, dst, d):
            return send(stage, src.at[partner(d)], part(dst, z), out_send, out_recv, d)

        @pl.loop(0, nz - 1)
        def _(step):
            far = nz // 2 - (step + 1) // 2
            odd = lax.rem(step, 2)
            d = far * odd + (nz - far) * (1 - odd)
            make(partner(d))
            for stage, src, dst in ways:
                back(stage, src, dst, d).start()

        make(z)
        mine = [keep(src.at[z], part(dst, z), 4 + stage) for stage, src, dst in ways]
        for c in mine:
            c.start()
        return [back(stage, src, dst, d) for stage, src, dst in ways for d in order] + mine

    vouts = return_all(value_grad, [(0, o1, gvt)])

    for c in thirds:
        c.wait()
    hop3 = hop(2, r3)
    for c in hop3:
        c.start()

    def lay_values(*sets):
        @pl.loop(0, nz)
        def _(i):
            for n in sets:
                lay(n, fv, i, r3)

    def score_grad_row(n, i):
        dw = jnp.sum(fg[n, i][None] * fv[n], axis=1)
        w = fw[n, i]
        low = w.astype(BF).astype(F32)
        dot = jnp.sum(low * dw, axis=0, keepdims=True)
        ds = (w * (dw - dot)).astype(BF).astype(F32)
        fd[n, i] = jnp.broadcast_to(ds[:, None, :], (nz, 8, LANES))

    lay_values(1)

    @pl.loop(0, nz)
    def _(i):
        score_grad_row(1, i)

    for c in hop3:
        c.wait()
    lay_values(0, 2)

    def query_grad(i):
        score_grad_row(0, i)
        score_grad_row(2, i)
        parts = [sum_over(lambda j: fk[n, j], lambda j: fd[n, i, j]) for n in range(3)]
        o2[0, i] = (choose(i, *parts) * SCALE).astype(BF)

    def key_grad(j):
        parts = [sum_over(lambda i: fq[n, i], lambda i: fd[n, i, j]) for n in range(3)]
        o2[1, j] = (choose(j, *parts) * SCALE).astype(BF)

    qkouts = return_all(query_grad, [(1, o2.at[0], gqt)])
    qkouts += return_all(key_grad, [(2, o2.at[1], gkt)])
    for c in vouts + qkouts + leaving:
        c.wait()


def hand_over(*refs):
    ins, outs, held, sems = refs[:6], refs[6:12], refs[12:18], refs[18]
    pulls = [pltpu.make_async_copy(a, b, sems.at[0, i]) for i, (a, b) in enumerate(zip(ins, held))]
    pushes = [pltpu.make_async_copy(a, b, sems.at[1, i]) for i, (a, b) in enumerate(zip(held, outs))]
    for c in pulls:
        c.start()
    for c, d in zip(pulls, pushes):
        c.wait()
        d.start()
    for c in pushes:
        c.wait()


def solution(mesh):
    nz, ng = mesh.shape["seq"], mesh.shape["grp"]

    def shards(*args):
        clip_len = args[8]
        _, tokens, channels = args[0].shape
        flat = [jnp.swapaxes(a[0], 0, 1).reshape(HEADS, HDIM, tokens) for a in args[:8]]
        anywhere = pl.BlockSpec(memory_space=pl.ANY)
        dma = pltpu.SemaphoreType.DMA
        frame = (HEADS, HDIM, tokens)
        outs = [jax.ShapeDtypeStruct(frame, BF)] * 6
        res = pl.pallas_call(
            functools.partial(kernel, nz, ng),
            out_shape=outs,
            in_specs=[anywhere] * 9,
            out_specs=[anywhere] * 6,
            scratch_shapes=[pltpu.VMEM(frame, BF)] * 4
            + [
                pltpu.VMEM((3, nz, 2, HDIM, LANES), BF),
                pltpu.VMEM((3, nz, HDIM, LANES), BF),
                pltpu.VMEM((3, nz, HDIM, LANES), BF),
                pltpu.VMEM((nz, HDIM, LANES), BF),
                pltpu.VMEM((2, nz, HDIM, LANES), BF),
                pltpu.VMEM((3, nz, HDIM, LANES), F32),
                pltpu.VMEM((3, nz, HDIM, LANES), F32),
                pltpu.VMEM((3, nz, HDIM, LANES), F32),
                pltpu.VMEM((3, nz, HDIM, LANES), F32),
                pltpu.VMEM((3, nz, nz, LANES), F32),
                pltpu.VMEM((3, nz, nz, 8, LANES), F32),
                pltpu.VMEM((3, nz, nz, 8, LANES), F32),
                pltpu.VMEM((3, nz, LANES), F32),
                pltpu.VMEM((2, nz, 8, LANES), F32),
                dma((5,)), dma((4, nz)), dma((4, nz)), dma((3, 2)), dma((3, 2)),
                dma((3, nz)), dma((3, nz)), dma((7,)), dma((3,)),
                pltpu.SemaphoreType.REGULAR((len(REACHES) - 1,)),
                pltpu.SemaphoreType.REGULAR((len(REACHES) - 1,)),
                pltpu.SMEM(clip_len.shape, clip_len.dtype),
            ],
            compiler_params=pltpu.CompilerParams(
                collective_id=0, has_side_effects=True, vmem_limit_bytes=63 << 20
            ),
        )(clip_len, *flat)
        res = pl.pallas_call(
            hand_over,
            out_shape=outs,
            in_specs=[anywhere] * 6,
            out_specs=[anywhere] * 6,
            scratch_shapes=[pltpu.VMEM(frame, BF)] * 6 + [dma((2, 6))],
            compiler_params=pltpu.CompilerParams(vmem_limit_bytes=63 << 20),
        )(*res)
        return tuple(jnp.swapaxes(r.reshape(channels, tokens), 0, 1)[None] for r in res)

    cut = P(("grp", "seq"), None, None)
    return jax.shard_map(
        shards, mesh=mesh, in_specs=(cut,) * 8 + (P(),), out_specs=(cut,) * 6, check_vma=False
    )
```

```python
import functools
import math

import jax
import jax.numpy as jnp
from jax import lax
from jax.experimental import pallas as pl
from jax.experimental.pallas import tpu as pltpu
from jax.sharding import PartitionSpec as P

HEADS = 8
HDIM = 72
LANES = 128
SCALE = 1.0 / math.sqrt(HDIM)
MASKED = -1e30
MESH = pl.DeviceIdType.MESH
REACHES = ((2, 0), (4, 2), (6, 2), (8, 2))
REACH = REACHES[0][0]
BF = jnp.bfloat16
F32 = jnp.float32


def space_head(h, qs, ks, vs, cs, gq, gk, gv):
    q, k, v, c = qs[h], ks[h], vs[h], cs[h]
    first = (((0,), (0,)), ((), ()))
    last = (((1,), (1,)), ((), ()))
    plain = (((1,), (0,)), ((), ()))
    scores = lax.dot_general(k, q, first, preferred_element_type=F32) * SCALE
    peak = jnp.max(scores, axis=0, keepdims=True)
    grown = jnp.exp(scores - peak)
    weights = grown * (1.0 / jnp.sum(grown, axis=0, keepdims=True))
    low = weights.astype(BF)
    dweights = lax.dot_general(v, c, first, preferred_element_type=F32)
    dot = jnp.sum(low.astype(F32) * dweights, axis=0, keepdims=True)
    dscores = (weights * (dweights - dot)).astype(BF)
    gq[h] = (lax.dot_general(k, dscores, plain, preferred_element_type=F32) * SCALE).astype(BF)
    gk[h] = (lax.dot_general(q, dscores, last, preferred_element_type=F32) * SCALE).astype(BF)
    gv[h] = lax.dot_general(c, low, last, preferred_element_type=F32).astype(BF)


def labels_of(clip_len, label, pick, nz, ng):
    g = lax.axis_index("grp")
    shape = (nz, LANES)
    slot = lax.broadcasted_iota(jnp.int32, shape, 0)
    ids = [slot + (g - 1 + n) * nz for n in range(3)]

    def count(c, carry):
        end, found = carry
        end = end + clip_len[c]
        return end, tuple(f + jnp.where(i >= end, 1, 0) for f, i in zip(found, ids))

    zero = jnp.zeros(shape, jnp.int32)
    _, found = lax.fori_loop(0, clip_len.shape[0], count, (jnp.int32(0), (zero,) * 3))
    low, own, high = [
        jnp.where((i >= 0) & (i < nz * ng), f, -1) for f, i in zip(found, ids)
    ]
    left = own == jnp.broadcast_to(low[nz - 1 : nz], shape)
    right = own == jnp.broadcast_to(high[0:1], shape)
    label[0] = jnp.where(left, own, low).astype(F32)
    label[1] = own.astype(F32)
    label[2] = jnp.where(right, own, high).astype(F32)
    for n, flag in ((0, left), (1, right)):
        pick[n] = jnp.broadcast_to(jnp.where(flag, 1.0, 0.0)[:, None, :], (nz, 8, LANES))


def kernel(
    nz, ng,
    clip_src, qs, ks, vs, cs, qt, kt, vt, ct,
    gqs, gks, gvs, gqt, gkt, gvt,
    iqs, iks, ivs, ics,
    r1, r2, r3, o1, o2,
    fq, fk, fv, fg, fw, fl, fd, labels, pick,
    bring, in_send, in_recv, hop_send, hop_recv, out_send, out_recv, self_sem, leave,
    right_in, left_in, clip_len,
):
    g = lax.axis_index("grp")
    z = lax.axis_index("seq")
    before = lax.rem(g + ng - 1, ng)
    after = lax.rem(g + 1, ng)

    def partner(d):
        return lax.rem(z + d, nz)

    def tell(sem, group, place):
        pl.semaphore_signal(sem, inc=1, device_id=(group, place), device_id_type=MESH)

    def part(ref, p):
        half = p // HEADS
        lanes = pl.ds(pl.multiple_of(half * LANES, LANES), LANES)
        return ref.at[p - half * HEADS, :, lanes]

    def send(stage, src, dst, sems_out, sems_in, d):
        return pltpu.make_async_remote_copy(
            src_ref=src, dst_ref=dst, send_sem=sems_out.at[stage, d],
            recv_sem=sems_in.at[stage, d], device_id=(g, partner(d)), device_id_type=MESH,
        )

    def bring_in(stage, ref, dst, d):
        return send(stage, part(ref, partner(d)), dst, in_send, in_recv, d)

    def keep(src, dst, i):
        return pltpu.make_async_copy(src, dst, self_sem.at[i])

    def hop(stage, ref):
        return [
            pltpu.make_async_remote_copy(
                src_ref=ref.at[1], dst_ref=ref.at[0], send_sem=hop_send.at[stage, 0],
                recv_sem=hop_recv.at[stage, 0], device_id=(after, z), device_id_type=MESH,
            ),
            pltpu.make_async_remote_copy(
                src_ref=ref.at[1], dst_ref=ref.at[2], send_sem=hop_send.at[stage, 1],
                recv_sem=hop_recv.at[stage, 1], device_id=(before, z), device_id_type=MESH,
            ),
        ]

    order = [nz // 2]
    for d in range(nz // 2 - 1, 0, -1):
        order += [d, nz - d]

    barrier = pltpu.get_barrier_semaphore()
    for d in range(REACH, 0, -1):
        tell(barrier, g, partner(d))
        tell(barrier, g, partner(nz - d))
    tell(barrier, before, z)
    tell(barrier, after, z)
    pairs = ((qs, iqs), (ks, iks), (vs, ivs), (cs, ics), (clip_src, clip_len))
    brought = [pltpu.make_async_copy(a, b, bring.at[i]) for i, (a, b) in enumerate(pairs)]
    own_first = [keep(part(qt, z), r1.at[1, z, 0], 0), keep(part(kt, z), r1.at[1, z, 1], 1)]
    pl.semaphore_wait(barrier, 2 * REACH + 2)

    known, rounds = 0, 0
    firsts = list(own_first)
    for limit, step in REACHES:
        if known:
            for way, far in ((right_in, nz - step), (left_in, step)):
                tell(way.at[rounds], g, partner(far))
            pl.semaphore_wait(right_in.at[rounds], 1)
            pl.semaphore_wait(left_in.at[rounds], 1)
            rounds += 1
        for k in range(limit, known, -1):
            for d in (k, nz - k) if k < nz - k else (k,):
                for which, ref in ((0, qt), (1, kt)):
                    copy = bring_in(which, ref, r1.at[1, z, which], d)
                    copy.start()
                    firsts.append(copy)
        if not known:
            for c in brought + own_first:
                c.start()
        known = limit
    for c in brought:
        c.wait()

    @pl.loop(0, HEADS)
    def _(h):
        space_head(h, iqs, iks, ivs, ics, iqs, iks, ivs)

    seconds = [keep(part(ct, z), r2.at[1, z], 2)]
    seconds += [bring_in(2, ct, r2.at[1, z], d) for d in order]
    for c in seconds:
        c.start()
    leaving = [
        pltpu.make_async_copy(a, b, leave.at[i])
        for i, (a, b) in enumerate(((iqs, gqs), (iks, gks), (ivs, gvs)))
    ]
    for c in leaving:
        c.start()
    labels_of(clip_len, labels, pick, nz, ng)
    for c in firsts:
        c.wait()
    hop1 = hop(0, r1)
    for c in hop1:
        c.start()
    thirds = [keep(part(vt, z), r3.at[1, z], 3)]
    thirds += [bring_in(3, vt, r3.at[1, z], d) for d in order]
    for c in thirds:
        c.start()

    def lay(n, target, row, ref, *which):
        mine = ref[(1, row) + which].astype(F32)
        if n == 1:
            target[1, row] = mine
        else:
            other = ref[(n, row) + which].astype(F32)
            target[n, row] = jnp.where(pick[n // 2, row, 0:1, :] > 0.5, mine, other)

    def scores_of(n):
        label = labels[n]

        @pl.loop(0, nz)
        def _(i):
            s = jnp.sum(fq[n, i][None] * fk[n], axis=1) * SCALE
            same = label == labels[n, pl.ds(i, 1), :]
            s = jnp.where(same, s, MASKED)
            e = jnp.where(same, jnp.exp(s - jnp.max(s, axis=0, keepdims=True)), 0.0)
            w = e * (1.0 / jnp.sum(e, axis=0, keepdims=True))
            low = w.astype(BF).astype(F32)
            fw[n, i] = w
            fl[n, i] = jnp.broadcast_to(low[:, None, :], (nz, 8, LANES))

    def sum_over(rows, coef):
        acc = jnp.zeros((HDIM // 8, 8, LANES), F32)
        for m in range(nz):
            acc = acc + rows(m).reshape(HDIM // 8, 8, LANES) * coef(m)[None]
        return acc.reshape(HDIM, LANES)

    @pl.loop(0, nz)
    def _(i):
        lay(1, fq, i, r1, 0)
        lay(1, fk, i, r1, 1)

    scores_of(1)
    for c in hop1:
        c.wait()

    for c in seconds:
        c.wait()
    hop2 = hop(1, r2)
    for c in hop2:
        c.start()

    @pl.loop(0, nz)
    def _(i):
        for n in (0, 2):
            lay(n, fq, i, r1, 0)
            lay(n, fk, i, r1, 1)

    scores_of(0)
    scores_of(2)

    @pl.loop(0, nz)
    def _(i):
        lay(1, fg, i, r2)

    for c in hop2:
        c.wait()

    @pl.loop(0, nz)
    def _(i):
        for n in (0, 2):
            lay(n, fg, i, r2)

    def choose(j, a, b, c):
        left = pick[0, j, 0:1, :] > 0.5
        right = pick[1, j, 0:1, :] > 0.5
        return jnp.where(left, a, jnp.where(right, c, b))

    def value_grad(j):
        parts = [sum_over(lambda i: fg[n, i], lambda i: fl[n, i, j]) for n in range(3)]
        o1[j] = choose(j, *parts).astype(BF)

    def return_all(make, ways):
        def back(stage, src, dst, d):
            return send(stage, src.at[partner(d)], part(dst, z), out_send, out_recv, d)

        @pl.loop(0, nz - 1)
        def _(step):
            far = nz // 2 - (step + 1) // 2
            odd = lax.rem(step, 2)
            d = far * odd + (nz - far) * (1 - odd)
            make(partner(d))
            for stage, src, dst in ways:
                back(stage, src, dst, d).start()

        make(z)
        mine = [keep(src.at[z], part(dst, z), 4 + stage) for stage, src, dst in ways]
        for c in mine:
            c.start()
        return [back(stage, src, dst, d) for stage, src, dst in ways for d in order] + mine

    vouts = return_all(value_grad, [(0, o1, gvt)])

    for c in thirds:
        c.wait()
    hop3 = hop(2, r3)
    for c in hop3:
        c.start()

    def lay_values(*sets):
        @pl.loop(0, nz)
        def _(i):
            for n in sets:
                lay(n, fv, i, r3)

    def score_grad_row(n, i):
        dw = jnp.sum(fg[n, i][None] * fv[n], axis=1)
        w = fw[n, i]
        low = w.astype(BF).astype(F32)
        dot = jnp.sum(low * dw, axis=0, keepdims=True)
        ds = (w * (dw - dot)).astype(BF).astype(F32)
        fd[n, i] = jnp.broadcast_to(ds[:, None, :], (nz, 8, LANES))

    lay_values(1)

    @pl.loop(0, nz)
    def _(i):
        score_grad_row(1, i)

    for c in hop3:
        c.wait()
    lay_values(0, 2)

    def query_grad(i):
        score_grad_row(0, i)
        score_grad_row(2, i)
        parts = [sum_over(lambda j: fk[n, j], lambda j: fd[n, i, j]) for n in range(3)]
        o2[0, i] = (choose(i, *parts) * SCALE).astype(BF)

    def key_grad(j):
        parts = [sum_over(lambda i: fq[n, i], lambda i: fd[n, i, j]) for n in range(3)]
        o2[1, j] = (choose(j, *parts) * SCALE).astype(BF)

    qkouts = return_all(query_grad, [(1, o2.at[0], gqt)])
    qkouts += return_all(key_grad, [(2, o2.at[1], gkt)])
    for c in vouts + qkouts + leaving:
        c.wait()


def hand_over(*refs):
    ins, outs, held, sems = refs[:6], refs[6:12], refs[12:18], refs[18]
    pulls = [pltpu.make_async_copy(a, b, sems.at[0, i]) for i, (a, b) in enumerate(zip(ins, held))]
    pushes = [pltpu.make_async_copy(a, b, sems.at[1, i]) for i, (a, b) in enumerate(zip(held, outs))]
    for c in pulls:
        c.start()
    for c, d in zip(pulls, pushes):
        c.wait()
        d.start()
    for c in pushes:
        c.wait()


def solution(mesh):
    nz, ng = mesh.shape["seq"], mesh.shape["grp"]

    def shards(*args):
        clip_len = args[8]
        _, tokens, channels = args[0].shape
        flat = [jnp.swapaxes(a[0], 0, 1).reshape(HEADS, HDIM, tokens) for a in args[:8]]
        anywhere = pl.BlockSpec(memory_space=pl.ANY)
        dma = pltpu.SemaphoreType.DMA
        frame = (HEADS, HDIM, tokens)
        outs = [jax.ShapeDtypeStruct(frame, BF)] * 6
        res = pl.pallas_call(
            functools.partial(kernel, nz, ng),
            out_shape=outs,
            in_specs=[anywhere] * 9,
            out_specs=[anywhere] * 6,
            scratch_shapes=[pltpu.VMEM(frame, BF)] * 4
            + [
                pltpu.VMEM((3, nz, 2, HDIM, LANES), BF),
                pltpu.VMEM((3, nz, HDIM, LANES), BF),
                pltpu.VMEM((3, nz, HDIM, LANES), BF),
                pltpu.VMEM((nz, HDIM, LANES), BF),
                pltpu.VMEM((2, nz, HDIM, LANES), BF),
                pltpu.VMEM((3, nz, HDIM, LANES), F32),
                pltpu.VMEM((3, nz, HDIM, LANES), F32),
                pltpu.VMEM((3, nz, HDIM, LANES), F32),
                pltpu.VMEM((3, nz, HDIM, LANES), F32),
                pltpu.VMEM((3, nz, nz, LANES), F32),
                pltpu.VMEM((3, nz, nz, 8, LANES), F32),
                pltpu.VMEM((3, nz, nz, 8, LANES), F32),
                pltpu.VMEM((3, nz, LANES), F32),
                pltpu.VMEM((2, nz, 8, LANES), F32),
                dma((5,)), dma((4, nz)), dma((4, nz)), dma((3, 2)), dma((3, 2)),
                dma((3, nz)), dma((3, nz)), dma((7,)), dma((3,)),
                pltpu.SemaphoreType.REGULAR((len(REACHES) - 1,)),
                pltpu.SemaphoreType.REGULAR((len(REACHES) - 1,)),
                pltpu.SMEM(clip_len.shape, clip_len.dtype),
            ],
            compiler_params=pltpu.CompilerParams(
                collective_id=0, has_side_effects=True, vmem_limit_bytes=63 << 20
            ),
        )(clip_len, *flat)
        res = pl.pallas_call(
            hand_over,
            out_shape=outs,
            in_specs=[anywhere] * 6,
            out_specs=[anywhere] * 6,
            scratch_shapes=[pltpu.VMEM(frame, BF)] * 6 + [dma((2, 6))],
            compiler_params=pltpu.CompilerParams(vmem_limit_bytes=63 << 20),
        )(*res)
        return tuple(jnp.swapaxes(r.reshape(channels, tokens), 0, 1)[None] for r in res)

    cut = P(("grp", "seq"), None, None)
    return jax.shard_map(
        shards, mesh=mesh, in_specs=(cut,) * 8 + (P(),), out_specs=(cut,) * 6, check_vma=False
    )
```

```python
import functools
import math

import jax
import jax.numpy as jnp
from jax import lax
from jax.experimental import pallas as pl
from jax.experimental.pallas import tpu as pltpu
from jax.sharding import PartitionSpec as P

HEADS = 8
HDIM = 72
LANES = 128
SCALE = 1.0 / math.sqrt(HDIM)
MASKED = -1e30
MESH = pl.DeviceIdType.MESH
REACHES = ((2, 0), (4, 2), (6, 2), (8, 2))
REACH = REACHES[0][0]
BF = jnp.bfloat16
F32 = jnp.float32


def space_head(h, qs, ks, vs, cs, gq, gk, gv):
    q, k, v, c = qs[h], ks[h], vs[h], cs[h]
    first = (((0,), (0,)), ((), ()))
    last = (((1,), (1,)), ((), ()))
    plain = (((1,), (0,)), ((), ()))
    scores = lax.dot_general(k, q, first, preferred_element_type=F32) * SCALE
    peak = jnp.max(scores, axis=0, keepdims=True)
    grown = jnp.exp(scores - peak)
    weights = grown * (1.0 / jnp.sum(grown, axis=0, keepdims=True))
    low = weights.astype(BF)
    dweights = lax.dot_general(v, c, first, preferred_element_type=F32)
    dot = jnp.sum(low.astype(F32) * dweights, axis=0, keepdims=True)
    dscores = (weights * (dweights - dot)).astype(BF)
    gq[h] = (lax.dot_general(k, dscores, plain, preferred_element_type=F32) * SCALE).astype(BF)
    gk[h] = (lax.dot_general(q, dscores, last, preferred_element_type=F32) * SCALE).astype(BF)
    gv[h] = lax.dot_general(c, low, last, preferred_element_type=F32).astype(BF)


def labels_of(clip_len, label, pick, nz, ng):
    g = lax.axis_index("grp")
    shape = (nz, LANES)
    slot = lax.broadcasted_iota(jnp.int32, shape, 0)
    ids = [slot + (g - 1 + n) * nz for n in range(3)]

    def count(c, carry):
        end, found = carry
        end = end + clip_len[c]
        return end, tuple(f + jnp.where(i >= end, 1, 0) for f, i in zip(found, ids))

    zero = jnp.zeros(shape, jnp.int32)
    _, found = lax.fori_loop(0, clip_len.shape[0], count, (jnp.int32(0), (zero,) * 3))
    low, own, high = [
        jnp.where((i >= 0) & (i < nz * ng), f, -1) for f, i in zip(found, ids)
    ]
    left = own == jnp.broadcast_to(low[nz - 1 : nz], shape)
    right = own == jnp.broadcast_to(high[0:1], shape)
    label[0] = jnp.where(left, own, low).astype(F32)
    label[1] = own.astype(F32)
    label[2] = jnp.where(right, own, high).astype(F32)
    for n, flag in ((0, left), (1, right)):
        pick[n] = jnp.broadcast_to(jnp.where(flag, 1.0, 0.0)[:, None, :], (nz, 8, LANES))


def kernel(
    nz, ng,
    clip_src, qs, ks, vs, cs, qt, kt, vt, ct,
    gqs, gks, gvs, gqt, gkt, gvt,
    iqs, iks, ivs, ics,
    r1, r2, r3, o1, o2,
    fq, fk, fv, fg, fw, fl, fd, labels, pick,
    bring, in_send, in_recv, hop_send, hop_recv, out_send, out_recv, self_sem, leave,
    right_in, left_in, clip_len,
):
    g = lax.axis_index("grp")
    z = lax.axis_index("seq")
    before = lax.rem(g + ng - 1, ng)
    after = lax.rem(g + 1, ng)

    def partner(d):
        return lax.rem(z + d, nz)

    def tell(sem, group, place):
        pl.semaphore_signal(sem, inc=1, device_id=(group, place), device_id_type=MESH)

    def part(ref, p):
        half = p // HEADS
        lanes = pl.ds(pl.multiple_of(half * LANES, LANES), LANES)
        return ref.at[p - half * HEADS, :, lanes]

    def send(stage, src, dst, sems_out, sems_in, d):
        return pltpu.make_async_remote_copy(
            src_ref=src, dst_ref=dst, send_sem=sems_out.at[stage, d],
            recv_sem=sems_in.at[stage, d], device_id=(g, partner(d)), device_id_type=MESH,
        )

    def bring_in(stage, ref, dst, d):
        return send(stage, part(ref, partner(d)), dst, in_send, in_recv, d)

    def keep(src, dst, i):
        return pltpu.make_async_copy(src, dst, self_sem.at[i])

    def hop(stage, ref):
        return [
            pltpu.make_async_remote_copy(
                src_ref=ref.at[1], dst_ref=ref.at[0], send_sem=hop_send.at[stage, 0],
                recv_sem=hop_recv.at[stage, 0], device_id=(after, z), device_id_type=MESH,
            ),
            pltpu.make_async_remote_copy(
                src_ref=ref.at[1], dst_ref=ref.at[2], send_sem=hop_send.at[stage, 1],
                recv_sem=hop_recv.at[stage, 1], device_id=(before, z), device_id_type=MESH,
            ),
        ]

    order = [nz // 2]
    for d in range(nz // 2 - 1, 0, -1):
        order += [d, nz - d]

    barrier = pltpu.get_barrier_semaphore()
    for d in range(REACH, 0, -1):
        tell(barrier, g, partner(d))
        tell(barrier, g, partner(nz - d))
    tell(barrier, before, z)
    tell(barrier, after, z)
    pairs = ((qs, iqs), (ks, iks), (vs, ivs), (cs, ics), (clip_src, clip_len))
    brought = [pltpu.make_async_copy(a, b, bring.at[i]) for i, (a, b) in enumerate(pairs)]
    own_first = [keep(part(qt, z), r1.at[1, z, 0], 0), keep(part(kt, z), r1.at[1, z, 1], 1)]
    pl.semaphore_wait(barrier, 2 * REACH + 2)

    known, rounds = 0, 0
    firsts = list(own_first)
    for limit, step in REACHES:
        if known:
            for way, far in ((right_in, nz - step), (left_in, step)):
                tell(way.at[rounds], g, partner(far))
            pl.semaphore_wait(right_in.at[rounds], 1)
            pl.semaphore_wait(left_in.at[rounds], 1)
            rounds += 1
        for k in range(limit, known, -1):
            for d in (k, nz - k) if k < nz - k else (k,):
                for which, ref in ((0, qt), (1, kt)):
                    copy = bring_in(which, ref, r1.at[1, z, which], d)
                    copy.start()
                    firsts.append(copy)
        if not known:
            for c in brought + own_first:
                c.start()
        known = limit
    seconds = [keep(part(ct, z), r2.at[1, z], 2)]
    seconds += [bring_in(2, ct, r2.at[1, z], d) for d in order]
    for c in seconds:
        c.start()
    for c in brought:
        c.wait()

    @pl.loop(0, HEADS)
    def _(h):
        space_head(h, iqs, iks, ivs, ics, iqs, iks, ivs)

    leaving = [
        pltpu.make_async_copy(a, b, leave.at[i])
        for i, (a, b) in enumerate(((iqs, gqs), (iks, gks), (ivs, gvs)))
    ]
    for c in leaving:
        c.start()
    labels_of(clip_len, labels, pick, nz, ng)
    for c in firsts:
        c.wait()
    hop1 = hop(0, r1)
    for c in hop1:
        c.start()
    thirds = [keep(part(vt, z), r3.at[1, z], 3)]
    thirds += [bring_in(3, vt, r3.at[1, z], d) for d in order]
    for c in thirds:
        c.start()

    def lay(n, target, row, ref, *which):
        mine = ref[(1, row) + which].astype(F32)
        if n == 1:
            target[1, row] = mine
        else:
            other = ref[(n, row) + which].astype(F32)
            target[n, row] = jnp.where(pick[n // 2, row, 0:1, :] > 0.5, mine, other)

    def scores_of(n):
        label = labels[n]

        @pl.loop(0, nz)
        def _(i):
            s = jnp.sum(fq[n, i][None] * fk[n], axis=1) * SCALE
            same = label == labels[n, pl.ds(i, 1), :]
            s = jnp.where(same, s, MASKED)
            e = jnp.where(same, jnp.exp(s - jnp.max(s, axis=0, keepdims=True)), 0.0)
            w = e * (1.0 / jnp.sum(e, axis=0, keepdims=True))
            low = w.astype(BF).astype(F32)
            fw[n, i] = w
            fl[n, i] = jnp.broadcast_to(low[:, None, :], (nz, 8, LANES))

    def sum_over(rows, coef):
        acc = jnp.zeros((HDIM // 8, 8, LANES), F32)
        for m in range(nz):
            acc = acc + rows(m).reshape(HDIM // 8, 8, LANES) * coef(m)[None]
        return acc.reshape(HDIM, LANES)

    @pl.loop(0, nz)
    def _(i):
        lay(1, fq, i, r1, 0)
        lay(1, fk, i, r1, 1)

    scores_of(1)
    for c in hop1:
        c.wait()

    for c in seconds:
        c.wait()
    hop2 = hop(1, r2)
    for c in hop2:
        c.start()

    @pl.loop(0, nz)
    def _(i):
        for n in (0, 2):
            lay(n, fq, i, r1, 0)
            lay(n, fk, i, r1, 1)

    scores_of(0)
    scores_of(2)

    @pl.loop(0, nz)
    def _(i):
        lay(1, fg, i, r2)

    for c in hop2:
        c.wait()

    @pl.loop(0, nz)
    def _(i):
        for n in (0, 2):
            lay(n, fg, i, r2)

    def choose(j, a, b, c):
        left = pick[0, j, 0:1, :] > 0.5
        right = pick[1, j, 0:1, :] > 0.5
        return jnp.where(left, a, jnp.where(right, c, b))

    def value_grad(j):
        parts = [sum_over(lambda i: fg[n, i], lambda i: fl[n, i, j]) for n in range(3)]
        o1[j] = choose(j, *parts).astype(BF)

    def return_all(make, ways):
        def back(stage, src, dst, d):
            return send(stage, src.at[partner(d)], part(dst, z), out_send, out_recv, d)

        @pl.loop(0, nz - 1)
        def _(step):
            far = nz // 2 - (step + 1) // 2
            odd = lax.rem(step, 2)
            d = far * odd + (nz - far) * (1 - odd)
            make(partner(d))
            for stage, src, dst in ways:
                back(stage, src, dst, d).start()

        make(z)
        mine = [keep(src.at[z], part(dst, z), 4 + stage) for stage, src, dst in ways]
        for c in mine:
            c.start()
        return [back(stage, src, dst, d) for stage, src, dst in ways for d in order] + mine

    vouts = return_all(value_grad, [(0, o1, gvt)])

    for c in thirds:
        c.wait()
    hop3 = hop(2, r3)
    for c in hop3:
        c.start()

    def lay_values(*sets):
        @pl.loop(0, nz)
        def _(i):
            for n in sets:
                lay(n, fv, i, r3)

    def score_grad_row(n, i):
        dw = jnp.sum(fg[n, i][None] * fv[n], axis=1)
        w = fw[n, i]
        low = w.astype(BF).astype(F32)
        dot = jnp.sum(low * dw, axis=0, keepdims=True)
        ds = (w * (dw - dot)).astype(BF).astype(F32)
        fd[n, i] = jnp.broadcast_to(ds[:, None, :], (nz, 8, LANES))

    lay_values(1)

    @pl.loop(0, nz)
    def _(i):
        score_grad_row(1, i)

    for c in hop3:
        c.wait()
    lay_values(0, 2)

    def query_grad(i):
        score_grad_row(0, i)
        score_grad_row(2, i)
        parts = [sum_over(lambda j: fk[n, j], lambda j: fd[n, i, j]) for n in range(3)]
        o2[0, i] = (choose(i, *parts) * SCALE).astype(BF)

    def key_grad(j):
        parts = [sum_over(lambda i: fq[n, i], lambda i: fd[n, i, j]) for n in range(3)]
        o2[1, j] = (choose(j, *parts) * SCALE).astype(BF)

    qkouts = return_all(query_grad, [(1, o2.at[0], gqt)])
    qkouts += return_all(key_grad, [(2, o2.at[1], gkt)])
    for c in vouts + qkouts + leaving:
        c.wait()


def hand_over(*refs):
    ins, outs, held, sems = refs[:6], refs[6:12], refs[12:18], refs[18]
    pulls = [pltpu.make_async_copy(a, b, sems.at[0, i]) for i, (a, b) in enumerate(zip(ins, held))]
    pushes = [pltpu.make_async_copy(a, b, sems.at[1, i]) for i, (a, b) in enumerate(zip(held, outs))]
    for c in pulls:
        c.start()
    for c, d in zip(pulls, pushes):
        c.wait()
        d.start()
    for c in pushes:
        c.wait()


def solution(mesh):
    nz, ng = mesh.shape["seq"], mesh.shape["grp"]

    def shards(*args):
        clip_len = args[8]
        _, tokens, channels = args[0].shape
        flat = [jnp.swapaxes(a[0], 0, 1).reshape(HEADS, HDIM, tokens) for a in args[:8]]
        anywhere = pl.BlockSpec(memory_space=pl.ANY)
        dma = pltpu.SemaphoreType.DMA
        frame = (HEADS, HDIM, tokens)
        outs = [jax.ShapeDtypeStruct(frame, BF)] * 6
        res = pl.pallas_call(
            functools.partial(kernel, nz, ng),
            out_shape=outs,
            in_specs=[anywhere] * 9,
            out_specs=[anywhere] * 6,
            scratch_shapes=[pltpu.VMEM(frame, BF)] * 4
            + [
                pltpu.VMEM((3, nz, 2, HDIM, LANES), BF),
                pltpu.VMEM((3, nz, HDIM, LANES), BF),
                pltpu.VMEM((3, nz, HDIM, LANES), BF),
                pltpu.VMEM((nz, HDIM, LANES), BF),
                pltpu.VMEM((2, nz, HDIM, LANES), BF),
                pltpu.VMEM((3, nz, HDIM, LANES), F32),
                pltpu.VMEM((3, nz, HDIM, LANES), F32),
                pltpu.VMEM((3, nz, HDIM, LANES), F32),
                pltpu.VMEM((3, nz, HDIM, LANES), F32),
                pltpu.VMEM((3, nz, nz, LANES), F32),
                pltpu.VMEM((3, nz, nz, 8, LANES), F32),
                pltpu.VMEM((3, nz, nz, 8, LANES), F32),
                pltpu.VMEM((3, nz, LANES), F32),
                pltpu.VMEM((2, nz, 8, LANES), F32),
                dma((5,)), dma((4, nz)), dma((4, nz)), dma((3, 2)), dma((3, 2)),
                dma((3, nz)), dma((3, nz)), dma((7,)), dma((3,)),
                pltpu.SemaphoreType.REGULAR((len(REACHES) - 1,)),
                pltpu.SemaphoreType.REGULAR((len(REACHES) - 1,)),
                pltpu.SMEM(clip_len.shape, clip_len.dtype),
            ],
            compiler_params=pltpu.CompilerParams(
                collective_id=0, has_side_effects=True, vmem_limit_bytes=63 << 20
            ),
        )(clip_len, *flat)
        res = pl.pallas_call(
            hand_over,
            out_shape=outs,
            in_specs=[anywhere] * 6,
            out_specs=[anywhere] * 6,
            scratch_shapes=[pltpu.VMEM(frame, BF)] * 6 + [dma((2, 6))],
            compiler_params=pltpu.CompilerParams(vmem_limit_bytes=63 << 20),
        )(*res)
        return tuple(jnp.swapaxes(r.reshape(channels, tokens), 0, 1)[None] for r in res)

    cut = P(("grp", "seq"), None, None)
    return jax.shard_map(
        shards, mesh=mesh, in_specs=(cut,) * 8 + (P(),), out_specs=(cut,) * 6, check_vma=False
    )
```
